32 devices in a mesh: row: 4 (over z), col: 2 (over x), layer: 4 (over y, core).
Axes of the slice: x: 2, y: 2, z: 4, core: 2. Of those that a mesh axis runs over, the one named last changes fastest.
Arguments:
- a_tiles: bfloat16 [4, 4, 2, 8, 4096], P('row', 'layer', 'col'), may hold values from -6 to 6
- b_tiles: bfloat16 [4, 4, 2, 16, 4096], P('layer', 'row', 'col'), may hold values from -0.25 to 0.25
- a_slots: int32 [4, 2, 4, 768], P('row', 'col', 'layer'), may hold values from 0 to 16, as said below
- b_slots: int32 [4, 2, 4, 768], P('row', 'col', 'layer'), may hold values from 0 to 63, as said below
Outputs:
- c_tiles: bfloat16 [4, 2, 96, 4096], P('row', 'col', 'layer')
The draws below stay inside these ranges and needn't reach their ends.
Inputs may be any that keep to these rules, and one draw needn't show every extreme that they name: `a_slots`: entries s * 8 to s * 8 + 7 are the tasks of product tile s; the value 16 marks a dummy task (the zero tile); a tile's live tasks come first, every tile has at least 2 live tasks, and in every list some tile has 8 live tasks and some tile has dummies. `b_slots`: A dummy task holds 0 here.
All inputs are finite; a program needn't handle non-finite values.
Results may differ from the reference program's by a relative error of at most 0.013.
Values may be sent and summed in bfloat16 or wider, within the bound.
No kernel may reach another device: no remote copies, remote signals or barrier semaphores. Data moves between devices by JAX's collectives and lax.ppermute only.
A program may use at most 128 MiB of HBM per device.

```python
import jax
import jax.numpy as jnp
from jax import lax

TILE = 64
TASKS = 8
TA = 8
TB = 16
TC = 96
N_ROW = 4
N_COL = 2
N_LAYER = 4


def live_entries(key):
    count_key, top_key, half_key = jax.random.split(key, 3)
    grid_shape = (N_ROW, N_COL, N_LAYER, TC)
    counts = jax.random.randint(count_key, grid_shape, TASKS // 4, TASKS + 1)
    top_place = jax.random.randint(top_key, (N_ROW, N_COL, N_LAYER, 1), 0, TC)
    half_place = (top_place + 1 + jax.random.randint(half_key, (N_ROW, N_COL, N_LAYER, 1), 0, TC - 1)) % TC
    tile_ids = jnp.arange(TC, dtype=jnp.int32)
    counts = jnp.where(tile_ids == half_place, TASKS // 2, counts)
    counts = jnp.where(tile_ids == top_place, TASKS, counts)
    entry_ids = jnp.arange(TASKS, dtype=jnp.int32)
    alive_mask = entry_ids < counts[..., None]
    return alive_mask.reshape(N_ROW, N_COL, N_LAYER, TC * TASKS)


def draw_a_slots(key, part):
    alive_mask = live_entries(key)
    key = jax.random.fold_in(key, 5)
    chosen = jax.random.randint(key, alive_mask.shape, 0, N_COL * TA)
    position = jnp.arange(TC * TASKS, dtype=jnp.int32)
    chosen = jnp.where(position == 0, 0, chosen)
    return jnp.where(alive_mask, chosen, N_COL * TA).astype(jnp.int32)


def draw_b_slots(key, part):
    alive_mask = live_entries(key)
    key = jax.random.fold_in(key, 9)
    chosen = jax.random.randint(key, alive_mask.shape, 0, N_ROW * TB)
    position = jnp.arange(TC * TASKS, dtype=jnp.int32)
    chosen = jnp.where(position == 0, N_ROW * TB - 1, chosen)
    return jnp.where(alive_mask, chosen, 0).astype(jnp.int32)


def level_of(key, extent, cuts, smallest, largest):
    gain, own = 1.0, jax.random.fold_in(key, 6)
    for dim, shards_of in cuts:
        heights = jnp.exp(jax.random.uniform(jax.random.fold_in(own, dim), (shards_of,), jnp.float32, smallest / len(cuts), largest / len(cuts)))
        gain = gain * jnp.repeat(heights, extent[dim] // shards_of).reshape([-1 if axis == dim else 1 for axis in range(len(extent))])
    return gain


def noise(rng, dims, spread, most, cuts=(), kind=jnp.bfloat16):
    level = level_of(rng, dims, cuts, -0.22, 0.18) if cuts else 1.0
    entries = jax.random.normal(rng, dims, jnp.float32) * spread * level
    return jnp.minimum(jnp.maximum(entries, -most), most).astype(kind)


def setup_inputs(seed: int = 0) -> dict:
    streams_of = jax.random.split(jax.random.key(seed), 5)
    return {
        "a_tiles": noise(streams_of[0], (N_ROW, N_LAYER, N_COL, TA, TILE * TILE), 1.0, 6.0, ((0, 4), (1, 4), (2, 2))),
        "b_tiles": noise(streams_of[1], (N_LAYER, N_ROW, N_COL, TB, TILE * TILE), (TASKS * TILE) ** -0.5, 0.25, ((0, 4), (1, 4), (2, 2))),
        "a_slots": draw_a_slots(jax.random.fold_in(streams_of[4], 71), 0),
        "b_slots": draw_b_slots(jax.random.fold_in(streams_of[4], 71), 0),
    }


def tile_sums(a_panel, b_panel, a_index, b_index):
    a_stack = a_panel[a_index].reshape(TC, TASKS, TILE, TILE).astype(jnp.float32)
    b_stack = b_panel[b_index].reshape(TC, TASKS, TILE, TILE).astype(jnp.float32)
    return jnp.einsum("sgik,sgkj->sij", a_stack, b_stack)


def reference(a_tiles, b_tiles, a_slots, b_slots):
    a_panels = a_tiles.reshape(N_ROW, N_LAYER, N_COL * TA, TILE, TILE)
    zero_tiles = jnp.zeros((N_ROW, N_LAYER, 1, TILE, TILE), a_tiles.dtype)
    a_panels = jnp.concatenate([a_panels, zero_tiles], axis=2)
    b_square = b_tiles.reshape(N_LAYER, N_ROW, N_COL, TB, TILE, TILE)
    b_panels = jnp.transpose(b_square, (0, 2, 1, 3, 4, 5)).reshape(N_LAYER, N_COL, N_ROW * TB, TILE, TILE)

    def one_panel(panel_id):
        grid_row = panel_id // N_COL
        grid_col = panel_id % N_COL
        running = jnp.zeros((TC, TILE, TILE), jnp.float32)
        for layer_part in range(N_LAYER):
            partial_value = tile_sums(a_panels[grid_row, layer_part], b_panels[layer_part, grid_col],
                                a_slots[grid_row, grid_col, layer_part], b_slots[grid_row, grid_col, layer_part])
            rounded = lax.optimization_barrier(partial_value.astype(jnp.bfloat16))
            running = running + rounded.astype(jnp.float32)
        return running.astype(jnp.bfloat16)

    c_all = lax.map(one_panel, jnp.arange(N_ROW * N_COL, dtype=jnp.int32))
    return c_all.reshape(N_ROW, N_COL, TC, TILE * TILE)
```

```python
import functools

import jax
import jax.numpy as jnp
from jax import lax
from jax.experimental import pallas as pl
from jax.experimental.pallas import tpu as pltpu
from jax.sharding import PartitionSpec as P

TILE = 64
TASKS = 8
FLAT = TILE * TILE
LANES = 128
LINES = FLAT // LANES
ROWS_AT_ONCE = 512
MIB = 1 << 20
F32, BF16 = jnp.float32, jnp.bfloat16
OWNER_ORDER = (0, 2, 3, 1)


def iota(shape, axis):
    return lax.broadcasted_iota(jnp.int32, shape, axis)


def split_inner_order():
    src, dst = iota((LANES, LANES), 0), iota((LANES, LANES), 1)
    half, rest = dst // TILE, dst % TILE
    wanted = half * TILE + 2 * (rest % (TILE // 2)) + rest // (TILE // 2)
    return jnp.where(src == wanted, 1.0, 0.0).astype(BF16)


def twice_on_diagonal(lines):
    low = iota(lines.shape, 1) < TILE
    turned = pltpu.roll(lines, TILE, 1)
    zero = jnp.zeros_like(lines)
    return jnp.concatenate(
        [
            jnp.where(low, lines, zero),
            jnp.where(low, turned, zero),
            jnp.where(low, zero, turned),
            jnp.where(low, zero, lines),
        ],
        axis=0,
    ).astype(BF16)


def loop(count, few, body):
    if count <= few:
        for i in range(count):
            body(i)
    else:
        pl.loop(0, count)(body)


def counts_kernel(swap, left_tiles, left_each, right_each, a_hbm, b_hbm, a_slots_hbm, b_slots_hbm, *refs):
    a_out, b_out, sel, a_slots, b_slots, sems = refs
    moves = [
        pltpu.make_async_copy(src, dst, sems.at[i])
        for i, (src, dst) in enumerate(
            ((a_slots_hbm, a_slots), (b_slots_hbm, b_slots), (a_hbm, a_out), (b_hbm, b_out))
        )
    ]
    for move in moves:
        move.start()
    row, col, layer = lax.axis_index("row"), lax.axis_index("col"), lax.axis_index("layer")
    tiles, pairs = sel.shape
    tasks = tiles * TASKS
    owned = tiles // len(OWNER_ORDER)
    place = iota((tiles, tasks), 0)
    group = place // owned
    owner = jnp.zeros_like(group)
    for g, q in enumerate(OWNER_ORDER):
        owner = jnp.where(group == g, q, owner)
    tile = (owner ^ layer) * owned + place % owned
    mine = jnp.where(iota((tiles, tasks), 1) // TASKS == tile, 1.0, 0.0).astype(BF16)
    entry = iota((2 * TASKS, tasks), 0)
    at = iota((2 * TASKS, tasks), 1) % TASKS
    moves[0].wait()
    moves[1].wait()
    a_index, b_index = a_slots[...], b_slots[...]
    a_place = a_index ^ (col * left_each) if swap else a_index
    a_place = jnp.where(a_index < left_tiles, a_place, left_tiles)
    b_place = ((b_index // right_each) ^ row) * right_each + b_index % right_each
    spread = jnp.where(at == entry, a_place, 0) + jnp.where(at + TASKS == entry, b_place, 0)
    lists = lax.dot_general(
        mine, spread.astype(F32).astype(BF16), (((1,), (1,)), ((), ())), preferred_element_type=F32
    ).astype(jnp.int32)
    width = min(pairs, 1024)

    def some(part):
        here = iota((tiles, width), 1) + part * width
        total = jnp.zeros((tiles, width), F32)
        for e in range(TASKS):
            a_at, b_at = lists[:, e:e + 1], lists[:, TASKS + e:TASKS + e + 1]
            pair = jnp.where(a_at < left_tiles, b_at * left_tiles + a_at, -1)
            total = total + jnp.where(here == pair, 1.0, 0.0)
        sel[:, pl.ds(pl.multiple_of(part * width, width), width)] = total.astype(BF16)

    loop(pairs // width, 1, some)
    moves[2].wait()
    moves[3].wait()


def left_lines(a_refs, a_lines):
    order = split_inner_order()
    left_tiles = sum(r.shape[0] for r in a_refs)
    lines_at_once = min(LINES, max(1, ROWS_AT_ONCE // left_tiles))
    for i in range(0, LINES, lines_at_once):
        block = jnp.concatenate(
            [
                r[:, j * LANES:(j + 1) * LANES].astype(F32)
                for j in range(i, i + lines_at_once)
                for r in a_refs
            ],
            axis=0,
        ).astype(BF16)
        got = jnp.dot(block, order, preferred_element_type=F32)
        a_lines[i * left_tiles:(i + lines_at_once) * left_tiles, :] = got.astype(BF16)


def all_products(a_lines, b_ref, raw, prod, first):
    right_tiles = b_ref.shape[0]
    left_tiles = a_lines.shape[0] // LINES
    for i in range(LINES):
        raw[i * right_tiles:(i + 1) * right_tiles, :] = b_ref[:, i * LANES:(i + 1) * LANES].astype(F32)
    lines_at_once = min(LINES, max(1, ROWS_AT_ONCE // left_tiles))
    rows = lines_at_once * left_tiles

    def pair(p):
        right = jnp.concatenate(
            [twice_on_diagonal(raw[pl.ds(2 * p + h, LINES, stride=right_tiles), :]) for h in range(2)], axis=1
        )

        def some(part):
            at = part * rows if isinstance(part, int) else pl.multiple_of(part * rows, rows)
            got = jnp.dot(a_lines[pl.ds(at, rows), :], right, preferred_element_type=F32).astype(BF16)
            for j in range(lines_at_once):
                for h in range(2):
                    to = first + (2 * p + h) * left_tiles
                    to = to if isinstance(to, int) else pl.multiple_of(to, left_tiles)
                    prod[part * lines_at_once + j, pl.ds(to, left_tiles), :] = got[
                        j * left_tiles:(j + 1) * left_tiles, h * LANES:(h + 1) * LANES
                    ]

        loop(LINES // lines_at_once, 1, some)

    loop(right_tiles // 2, 8 if rows == a_lines.shape[0] else 1, pair)


def chosen_sums(sel, first, count, prod, put):
    for j in range(0, LINES, 2):
        right = jnp.concatenate([prod[j, :count, :], prod[j + 1, :count, :]], axis=1)
        put(
            slice(j * LANES, (j + 2) * LANES),
            jnp.dot(sel[:, first:first + count], right, preferred_element_type=F32),
        )


def first_kernel(groups, n_left, sel, *refs):
    shards = sum(groups)
    a_refs, b_refs = refs[:n_left], refs[n_left:n_left + shards]
    acc, a_lines, raw, prod = refs[n_left + shards:]
    left_lines(a_refs, a_lines)
    pairs = b_refs[0].shape[0] * a_lines.shape[0] // LINES
    shard = 0
    for count in groups:
        start = shard
        for i in range(count):
            all_products(a_lines, b_refs[shard], raw, prod, i * pairs)
            shard += 1

        def put(columns, value):
            acc[:, columns] = value if start == 0 else acc[:, columns] + value

        chosen_sums(sel, start * pairs, count * pairs, prod, put)


def last_kernel(before, sel, a_lines, b_ref, acc, own, far, cross, near, raw, prod):
    pairs = b_ref.shape[0] * a_lines.shape[0] // LINES
    owned = own.shape[0]
    all_products(a_lines, b_ref, raw, prod, 0)

    def put(columns, value):
        value = value + acc[:, columns]
        for i, out in enumerate((own, far, cross, near)):
            out[:, columns] = value[i * owned:(i + 1) * owned].astype(out.dtype)

    chosen_sums(sel, before * pairs, pairs, prod, put)


def join_kernel(far, arrived, out):
    out[...] = (far[...] + arrived[...].astype(F32)).astype(out.dtype)


def add_kernel(own, arrived, joined, out):
    out[...] = (own[...] + arrived[...].astype(F32) + joined[...].astype(F32)).astype(out.dtype)


VMEM = pl.BlockSpec(memory_space=pltpu.VMEM)
HBM = pl.BlockSpec(memory_space=pltpu.HBM)


def shape(dims, kind):
    return jax.ShapeDtypeStruct(dims, kind)


def call(kernel, outs, scratch, n_in, name, flops, moved, place=VMEM, sems=()):
    held = sum(s.dtype.itemsize * functools.reduce(lambda x, y: x * y, s.shape) for s in outs + scratch)
    return pl.pallas_call(
        kernel,
        out_shape=outs,
        in_specs=[place] * n_in,
        out_specs=[VMEM] * len(outs),
        scratch_shapes=[pltpu.VMEM(s.shape, s.dtype) for s in scratch] + list(sems),
        compiler_params=pltpu.CompilerParams(vmem_limit_bytes=min(held + 16 * MIB, 58 * MIB)),
        cost_estimate=pl.CostEstimate(flops=flops, bytes_accessed=moved, transcendentals=0),
        name=name,
    )


def exchange(x, axis, q):
    size = lax.axis_size(axis)
    return lax.ppermute(x, axis, [(i, i ^ q) for i in range(size)])


def shards(a_tiles, b_tiles, a_slots, b_slots):
    a_local = a_tiles.reshape(-1, FLAT)
    b_local = b_tiles.reshape(-1, FLAT)
    a_index = a_slots.reshape(1, -1)
    b_index = b_slots.reshape(1, -1)
    rows, cols, layers = lax.axis_size("row"), lax.axis_size("col"), lax.axis_size("layer")
    left_each, right_each = a_local.shape[0], b_local.shape[0]
    left_tiles = cols * left_each
    tiles = a_index.shape[1] // TASKS
    owned = tiles // layers
    pairs = right_each * left_tiles
    assert rows == 4 and layers == len(OWNER_ORDER)

    b_far = exchange(b_local, "row", 2)
    if cols == 2:
        a_parts = [a_local, exchange(a_local, "col", 1)]
    else:
        a_parts = [lax.all_gather(a_local, "col", axis=0, tiled=True)]
    b_near = exchange(b_local, "row", 1)
    b_last = exchange(b_far, "row", 1)

    a_here, b_here, sel = call(
        functools.partial(counts_kernel, cols == 2, left_tiles, left_each, right_each),
        [
            shape(a_local.shape, BF16),
            shape(b_local.shape, BF16),
            shape((tiles, rows * pairs), BF16),
        ],
        [shape(a_index.shape, jnp.int32)] * 2,
        4,
        "counts",
        2 * tiles * tiles * TASKS * TASKS,
        2 * MIB,
        HBM,
        [pltpu.SemaphoreType.DMA((4,))],
    )(a_local, b_local, a_index, b_index)
    if cols == 2:
        a_parts[0] = a_here

    groups = (3,) if pairs * FLAT * 2 < 4 * MIB else (1, 1, 1)
    raw = shape((right_each * LINES, LANES), F32)
    shard_flops = 2 * pairs * LINES * LANES * LANES + 2 * pairs * tiles * FLAT
    acc, a_lines = call(
        functools.partial(first_kernel, groups, len(a_parts)),
        [shape((tiles, FLAT), F32), shape((left_tiles * LINES, LANES), BF16)],
        [raw, shape((LINES, max(groups) * pairs, LANES), BF16)],
        4 + len(a_parts),
        "own_and_near",
        3 * shard_flops,
        12 * MIB,
    )(sel, *a_parts, b_here, b_near, b_far)
    own, far, cross, near = call(
        functools.partial(last_kernel, 3),
        [shape((owned, FLAT), F32)] * 2 + [shape((owned, FLAT), BF16)] * 2,
        [raw, shape((LINES, pairs, LANES), BF16)],
        4,
        "last_shard",
        shard_flops,
        4 * MIB,
    )(sel, a_lines, b_last, acc)

    arrived_cross = exchange(cross, "layer", 1)
    arrived_near = exchange(near, "layer", 1)
    (joined,) = call(
        join_kernel, [shape((owned, FLAT), BF16)], [], 2, "join_cores", owned * FLAT, 1 * MIB
    )(far, arrived_cross)
    (out,) = call(
        add_kernel, [shape((owned, FLAT), BF16)], [], 3, "add_layers", 2 * owned * FLAT, 1 * MIB
    )(own, arrived_near, exchange(joined, "layer", 2))
    return out.reshape(1, 1, owned, FLAT)


def solution(mesh):
    in_specs = (
        P("row", "layer", "col", None, None),
        P("layer", "row", "col", None, None),
        P("row", "col", "layer", None),
        P("row", "col", "layer", None),
    )
    out_specs = P("row", "col", "layer", None)
    return jax.shard_map(shards, mesh=mesh, in_specs=in_specs, out_specs=out_specs, check_vma=False)
```

```python
import functools

import jax
import jax.numpy as jnp
from jax import lax
from jax.experimental import pallas as pl
from jax.experimental.pallas import tpu as pltpu
from jax.sharding import PartitionSpec as P

TILE = 64
TASKS = 8
FLAT = TILE * TILE
LANES = 128
LINES = FLAT // LANES
ROWS_AT_ONCE = 512
MIB = 1 << 20
STAGE_FLOPS = 2 * 10**9
F32, BF16 = jnp.float32, jnp.bfloat16
OWNER_ORDER = (0, 2, 3, 1)


def iota(shape, axis):
    return lax.broadcasted_iota(jnp.int32, shape, axis)


def split_inner_order():
    src, dst = iota((LANES, LANES), 0), iota((LANES, LANES), 1)
    half, rest = dst // TILE, dst % TILE
    wanted = half * TILE + 2 * (rest % (TILE // 2)) + rest // (TILE // 2)
    return jnp.where(src == wanted, 1.0, 0.0).astype(BF16)


def twice_on_diagonal(lines):
    low = iota(lines.shape, 1) < TILE
    turned = pltpu.roll(lines, TILE, 1)
    zero = jnp.zeros_like(lines)
    return jnp.concatenate(
        [
            jnp.where(low, lines, zero),
            jnp.where(low, turned, zero),
            jnp.where(low, zero, turned),
            jnp.where(low, zero, lines),
        ],
        axis=0,
    ).astype(BF16)


def loop(count, few, body):
    if count <= few:
        for i in range(count):
            body(i)
    else:
        pl.loop(0, count)(body)


def stage_kernel(b_ref, out, upper):
    out[...] = b_ref[...]
    upper[...] = b_ref[upper.shape[0]:, :]


def lower_kernel(b_ref, out):
    out[...] = b_ref[:out.shape[0], :]


def counts_kernel(swap, left_tiles, left_each, right_each, a_slots, b_slots, sel):
    row, col, layer = lax.axis_index("row"), lax.axis_index("col"), lax.axis_index("layer")
    tiles, pairs = sel.shape
    tasks = tiles * TASKS
    owned = tiles // len(OWNER_ORDER)
    place = iota((tiles, tasks), 0)
    group = place // owned
    owner = jnp.zeros_like(group)
    for g, q in enumerate(OWNER_ORDER):
        owner = jnp.where(group == g, q, owner)
    tile = (owner ^ layer) * owned + place % owned
    mine = jnp.where(iota((tiles, tasks), 1) // TASKS == tile, 1.0, 0.0).astype(BF16)
    entry = iota((2 * TASKS, tasks), 0)
    at = iota((2 * TASKS, tasks), 1) % TASKS
    a_index, b_index = a_slots[...], b_slots[...]
    a_place = a_index ^ (col * left_each) if swap else a_index
    a_place = jnp.where(a_index < left_tiles, a_place, left_tiles)
    b_place = ((b_index // right_each) ^ row) * right_each + b_index % right_each
    spread = jnp.where(at == entry, a_place, 0) + jnp.where(at + TASKS == entry, b_place, 0)
    lists = lax.dot_general(
        mine, spread.astype(F32).astype(BF16), (((1,), (1,)), ((), ())), preferred_element_type=F32
    ).astype(jnp.int32)
    width = min(pairs, 1024)

    def some(part):
        here = iota((tiles, width), 1) + part * width
        total = jnp.zeros((tiles, width), F32)
        for e in range(TASKS):
            a_at, b_at = lists[:, e:e + 1], lists[:, TASKS + e:TASKS + e + 1]
            pair = jnp.where(a_at < left_tiles, b_at * left_tiles + a_at, -1)
            total = total + jnp.where(here == pair, 1.0, 0.0)
        sel[:, pl.ds(pl.multiple_of(part * width, width), width)] = total.astype(BF16)

    loop(pairs // width, 1, some)


def left_lines(a_refs, a_lines):
    order = split_inner_order()
    left_tiles = sum(r.shape[0] for r in a_refs)
    lines_at_once = min(LINES, max(1, ROWS_AT_ONCE // left_tiles))
    for i in range(0, LINES, lines_at_once):
        block = jnp.concatenate(
            [
                r[:, j * LANES:(j + 1) * LANES].astype(F32)
                for j in range(i, i + lines_at_once)
                for r in a_refs
            ],
            axis=0,
        ).astype(BF16)
        got = jnp.dot(block, order, preferred_element_type=F32)
        a_lines[i * left_tiles:(i + lines_at_once) * left_tiles, :] = got.astype(BF16)


def all_products(a_lines, b_ref, raw, prod, first):
    right_tiles = b_ref.shape[0]
    left_tiles = a_lines.shape[0] // LINES
    for i in range(LINES):
        raw[i * right_tiles:(i + 1) * right_tiles, :] = b_ref[:, i * LANES:(i + 1) * LANES].astype(F32)
    lines_at_once = min(LINES, max(1, ROWS_AT_ONCE // left_tiles))
    rows = lines_at_once * left_tiles

    def pair(p):
        right = jnp.concatenate(
            [twice_on_diagonal(raw[pl.ds(2 * p + h, LINES, stride=right_tiles), :]) for h in range(2)], axis=1
        )

        def some(part):
            at = part * rows if isinstance(part, int) else pl.multiple_of(part * rows, rows)
            got = jnp.dot(a_lines[pl.ds(at, rows), :], right, preferred_element_type=F32).astype(BF16)
            for j in range(lines_at_once):
                for h in range(2):
                    to = first + (2 * p + h) * left_tiles
                    to = to if isinstance(to, int) else pl.multiple_of(to, left_tiles)
                    prod[part * lines_at_once + j, pl.ds(to, left_tiles), :] = got[
                        j * left_tiles:(j + 1) * left_tiles, h * LANES:(h + 1) * LANES
                    ]

        loop(LINES // lines_at_once, 1, some)

    loop(right_tiles // 2, 8 if rows == a_lines.shape[0] else 1, pair)


def chosen_sums(sel, first, count, prod, put):
    for j in range(0, LINES, 2):
        right = jnp.concatenate([prod[j, :count, :], prod[j + 1, :count, :]], axis=1)
        put(
            slice(j * LANES, (j + 2) * LANES),
            jnp.dot(sel[:, first:first + count], right, preferred_element_type=F32),
        )


def first_kernel(groups, n_left, sel, *refs):
    shards = sum(groups)
    a_refs, b_refs = refs[:n_left], refs[n_left:n_left + shards]
    acc, a_lines, raw, prod = refs[n_left + shards:]
    left_lines(a_refs, a_lines)
    pairs = b_refs[0].shape[0] * a_lines.shape[0] // LINES
    shard = 0
    for count in groups:
        start = shard
        for i in range(count):
            all_products(a_lines, b_refs[shard], raw, prod, i * pairs)
            shard += 1

        def put(columns, value):
            acc[:, columns] = value if start == 0 else acc[:, columns] + value

        chosen_sums(sel, start * pairs, count * pairs, prod, put)


def last_kernel(start, n_parts, sel, a_lines, acc, *refs):
    b_refs, (own, far, cross, near, raw, prod) = refs[:n_parts], refs[n_parts:]
    each = a_lines.shape[0] // LINES
    owned = own.shape[0]
    done = 0
    for b_ref in b_refs:
        all_products(a_lines, b_ref, raw, prod, done)
        done += b_ref.shape[0] * each

    def put(columns, value):
        value = value + acc[:, columns]
        for i, out in enumerate((own, far, cross, near)):
            out[:, columns] = value[i * owned:(i + 1) * owned].astype(out.dtype)

    chosen_sums(sel, start, done, prod, put)


def join_kernel(far, arrived, out):
    out[...] = (far[...] + arrived[...].astype(F32)).astype(out.dtype)


def add_kernel(own, arrived, joined, out):
    out[...] = (own[...] + arrived[...].astype(F32) + joined[...].astype(F32)).astype(out.dtype)


VMEM = pl.BlockSpec(memory_space=pltpu.VMEM)


def shape(dims, kind):
    return jax.ShapeDtypeStruct(dims, kind)


def call(kernel, outs, scratch, n_in, name, flops, moved):
    held = sum(s.dtype.itemsize * functools.reduce(lambda x, y: x * y, s.shape) for s in outs + scratch)
    return pl.pallas_call(
        kernel,
        out_shape=outs,
        in_specs=[VMEM] * n_in,
        out_specs=[VMEM] * len(outs),
        scratch_shapes=[pltpu.VMEM(s.shape, s.dtype) for s in scratch],
        compiler_params=pltpu.CompilerParams(vmem_limit_bytes=min(held + 16 * MIB, 58 * MIB)),
        cost_estimate=pl.CostEstimate(flops=flops, bytes_accessed=moved, transcendentals=0),
        name=name,
    )


def exchange(x, axis, q):
    size = lax.axis_size(axis)
    return lax.ppermute(x, axis, [(i, i ^ q) for i in range(size)])


def shards(a_tiles, b_tiles, a_slots, b_slots):
    a_local = a_tiles.reshape(-1, FLAT)
    b_local = b_tiles.reshape(-1, FLAT)
    a_index = a_slots.reshape(1, -1)
    b_index = b_slots.reshape(1, -1)
    rows, cols, layers = lax.axis_size("row"), lax.axis_size("col"), lax.axis_size("layer")
    left_each, right_each = a_local.shape[0], b_local.shape[0]
    left_tiles = cols * left_each
    tiles = a_index.shape[1] // TASKS
    owned = tiles // layers
    pairs = right_each * left_tiles
    assert rows == 4 and layers == len(OWNER_ORDER)

    b_far = exchange(b_local, "row", 2)
    if cols == 2:
        a_parts = [a_local, exchange(a_local, "col", 1)]
    else:
        a_parts = [lax.all_gather(a_local, "col", axis=0, tiled=True)]
    upper = right_each // 2
    b_here, b_upper = call(
        stage_kernel,
        [shape(b_local.shape, BF16), shape((upper, FLAT), BF16)],
        [],
        1,
        "stage",
        STAGE_FLOPS,
        MIB,
    )(b_local)
    b_near = exchange(b_here, "row", 1)
    last_upper = exchange(b_upper, "row", 3)
    (sel,) = call(
        functools.partial(counts_kernel, cols == 2, left_tiles, left_each, right_each),
        [shape((tiles, rows * pairs), BF16)],
        [],
        2,
        "counts",
        2 * tiles * tiles * TASKS * TASKS,
        MIB,
    )(a_index, b_index)
    (b_lower,) = call(lower_kernel, [shape((right_each - upper, FLAT), BF16)], [], 1, "lower", upper * FLAT, MIB)(b_far)
    last_lower = exchange(b_lower, "row", 1)

    groups = (3,) if pairs * FLAT * 2 < 4 * MIB else (1, 1, 1)
    raw = shape((right_each * LINES, LANES), F32)
    half_raw = shape((upper * LINES, LANES), F32)
    shard_flops = 2 * pairs * LINES * LANES * LANES + 2 * pairs * tiles * FLAT
    acc, a_lines = call(
        functools.partial(first_kernel, groups, len(a_parts)),
        [shape((tiles, FLAT), F32), shape((left_tiles * LINES, LANES), BF16)],
        [raw, shape((LINES, max(groups) * pairs, LANES), BF16)],
        4 + len(a_parts),
        "own_and_near",
        3 * shard_flops,
        12 * MIB,
    )(sel, *a_parts, b_here, b_near, b_far)
    own, far, cross, near = call(
        functools.partial(last_kernel, 3 * pairs, 2),
        [shape((owned, FLAT), F32)] * 2 + [shape((owned, FLAT), BF16)] * 2,
        [half_raw, shape((LINES, pairs, LANES), BF16)],
        5,
        "last_shard",
        shard_flops,
        4 * MIB,
    )(sel, a_lines, acc, last_lower, last_upper)

    arrived_cross = exchange(cross, "layer", 1)
    arrived_near = exchange(near, "layer", 1)
    (joined,) = call(
        join_kernel, [shape((owned, FLAT), BF16)], [], 2, "join_cores", owned * FLAT, 1 * MIB
    )(far, arrived_cross)
    (out,) = call(
        add_kernel, [shape((owned, FLAT), BF16)], [], 3, "add_layers", 2 * owned * FLAT, 1 * MIB
    )(own, arrived_near, exchange(joined, "layer", 2))
    return out.reshape(1, 1, owned, FLAT)


def solution(mesh):
    in_specs = (
        P("row", "layer", "col", None, None),
        P("layer", "row", "col", None, None),
        P("row", "col", "layer", None),
        P("row", "col", "layer", None),
    )
    out_specs = P("row", "col", "layer", None)
    return jax.shard_map(shards, mesh=mesh, in_specs=in_specs, out_specs=out_specs, check_vma=False)
```

```python
import functools

import jax
import jax.numpy as jnp
from jax import lax
from jax.experimental import pallas as pl
from jax.experimental.pallas import tpu as pltpu
from jax.sharding import PartitionSpec as P

TILE = 64
TASKS = 8
FLAT = TILE * TILE
LANES = 128
LINES = FLAT // LANES
ROWS_AT_ONCE = 512
MIB = 1 << 20
STAGE_FLOPS = 2 * 10**9
F32, BF16 = jnp.float32, jnp.bfloat16
OWNER_ORDER = (0, 2, 3, 1)


def iota(shape, axis):
    return lax.broadcasted_iota(jnp.int32, shape, axis)


def split_inner_order():
    src, dst = iota((LANES, LANES), 0), iota((LANES, LANES), 1)
    half, rest = dst // TILE, dst % TILE
    wanted = half * TILE + 2 * (rest % (TILE // 2)) + rest // (TILE // 2)
    return jnp.where(src == wanted, 1.0, 0.0).astype(BF16)


def twice_on_diagonal(lines):
    low = iota(lines.shape, 1) < TILE
    turned = pltpu.roll(lines, TILE, 1)
    zero = jnp.zeros_like(lines)
    return jnp.concatenate(
        [
            jnp.where(low, lines, zero),
            jnp.where(low, turned, zero),
            jnp.where(low, zero, turned),
            jnp.where(low, zero, lines),
        ],
        axis=0,
    ).astype(BF16)


def loop(count, few, body):
    if count <= few:
        for i in range(count):
            body(i)
    else:
        pl.loop(0, count)(body)


def stage_kernel(*refs):
    for ref, out in zip(refs[:len(refs) // 2], refs[len(refs) // 2:]):
        out[...] = ref[...]


def counts_kernel(swap, left_tiles, left_each, right_each, a_slots, b_slots, sel):
    row, col, layer = lax.axis_index("row"), lax.axis_index("col"), lax.axis_index("layer")
    tiles, pairs = sel.shape
    tasks = tiles * TASKS
    owned = tiles // len(OWNER_ORDER)
    place = iota((tiles, tasks), 0)
    group = place // owned
    owner = jnp.zeros_like(group)
    for g, q in enumerate(OWNER_ORDER):
        owner = jnp.where(group == g, q, owner)
    tile = (owner ^ layer) * owned + place % owned
    mine = jnp.where(iota((tiles, tasks), 1) // TASKS == tile, 1.0, 0.0).astype(BF16)
    entry = iota((2 * TASKS, tasks), 0)
    at = iota((2 * TASKS, tasks), 1) % TASKS
    a_index, b_index = a_slots[...], b_slots[...]
    a_place = a_index ^ (col * left_each) if swap else a_index
    a_place = jnp.where(a_index < left_tiles, a_place, left_tiles)
    b_place = ((b_index // right_each) ^ row) * right_each + b_index % right_each
    spread = jnp.where(at == entry, a_place, 0) + jnp.where(at + TASKS == entry, b_place, 0)
    lists = lax.dot_general(
        mine, spread.astype(F32).astype(BF16), (((1,), (1,)), ((), ())), preferred_element_type=F32
    ).astype(jnp.int32)
    width = min(pairs, 1024)

    def some(part):
        here = iota((tiles, width), 1) + part * width
        total = jnp.zeros((tiles, width), F32)
        for e in range(TASKS):
            a_at, b_at = lists[:, e:e + 1], lists[:, TASKS + e:TASKS + e + 1]
            pair = jnp.where(a_at < left_tiles, b_at * left_tiles + a_at, -1)
            total = total + jnp.where(here == pair, 1.0, 0.0)
        sel[:, pl.ds(pl.multiple_of(part * width, width), width)] = total.astype(BF16)

    loop(pairs // width, 1, some)


def left_lines(a_refs, a_lines):
    order = split_inner_order()
    left_tiles = sum(r.shape[0] for r in a_refs)
    lines_at_once = min(LINES, max(1, ROWS_AT_ONCE // left_tiles))
    for i in range(0, LINES, lines_at_once):
        block = jnp.concatenate(
            [
                r[:, j * LANES:(j + 1) * LANES].astype(F32)
                for j in range(i, i + lines_at_once)
                for r in a_refs
            ],
            axis=0,
        ).astype(BF16)
        got = jnp.dot(block, order, preferred_element_type=F32)
        a_lines[i * left_tiles:(i + lines_at_once) * left_tiles, :] = got.astype(BF16)


def all_products(a_lines, b_ref, raw, prod, first):
    right_tiles = b_ref.shape[0]
    left_tiles = a_lines.shape[0] // LINES
    for i in range(LINES):
        raw[i * right_tiles:(i + 1) * right_tiles, :] = b_ref[:, i * LANES:(i + 1) * LANES].astype(F32)
    lines_at_once = min(LINES, max(1, ROWS_AT_ONCE // left_tiles))
    rows = lines_at_once * left_tiles

    def pair(p):
        right = jnp.concatenate(
            [twice_on_diagonal(raw[pl.ds(2 * p + h, LINES, stride=right_tiles), :]) for h in range(2)], axis=1
        )

        def some(part):
            at = part * rows if isinstance(part, int) else pl.multiple_of(part * rows, rows)
            got = jnp.dot(a_lines[pl.ds(at, rows), :], right, preferred_element_type=F32).astype(BF16)
            for j in range(lines_at_once):
                for h in range(2):
                    to = first + (2 * p + h) * left_tiles
                    to = to if isinstance(to, int) else pl.multiple_of(to, left_tiles)
                    prod[part * lines_at_once + j, pl.ds(to, left_tiles), :] = got[
                        j * left_tiles:(j + 1) * left_tiles, h * LANES:(h + 1) * LANES
                    ]

        loop(LINES // lines_at_once, 1, some)

    loop(right_tiles // 2, 8 if rows == a_lines.shape[0] else 1, pair)


def chosen_sums(sel, first, count, prod, put):
    for j in range(0, LINES, 2):
        right = jnp.concatenate([prod[j, :count, :], prod[j + 1, :count, :]], axis=1)
        put(
            slice(j * LANES, (j + 2) * LANES),
            jnp.dot(sel[:, first:first + count], right, preferred_element_type=F32),
        )


def own_kernel(groups, n_left, sel, *refs):
    shards = sum(groups)
    a_refs, b_refs = refs[:n_left], refs[n_left:n_left + shards]
    acc, a_lines, raw, prod = refs[n_left + shards:]
    left_lines(a_refs, a_lines)
    add_shards(0, groups, sel, a_lines, b_refs, None, acc, raw, prod)


def more_kernel(start, sel, a_lines, acc, b_ref, out, raw, prod):
    add_shards(start, (1,), sel, a_lines, (b_ref,), acc, out, raw, prod)


def add_shards(start, groups, sel, a_lines, b_refs, acc, out, raw, prod):
    each = a_lines.shape[0] // LINES
    taken = 0
    for count in groups:
        done = 0
        before = out if taken else acc
        for b_ref in b_refs[taken:taken + count]:
            all_products(a_lines, b_ref, raw, prod, done)
            done += b_ref.shape[0] * each

        def put(columns, value):
            out[:, columns] = value if before is None else value + before[:, columns]

        chosen_sums(sel, start, done, prod, put)
        taken += count
        start += done


def last_kernel(start, sel, a_lines, acc, b_ref, own, far, cross, near, raw, prod):
    pairs = b_ref.shape[0] * a_lines.shape[0] // LINES
    owned = own.shape[0]
    all_products(a_lines, b_ref, raw, prod, 0)

    def put(columns, value):
        value = value + acc[:, columns]
        for i, out in enumerate((own, far, cross, near)):
            out[:, columns] = value[i * owned:(i + 1) * owned].astype(out.dtype)

    chosen_sums(sel, start, pairs, prod, put)


def join_kernel(far, arrived, out):
    out[...] = (far[...] + arrived[...].astype(F32)).astype(out.dtype)


def add_kernel(own, arrived, joined, out):
    out[...] = (own[...] + arrived[...].astype(F32) + joined[...].astype(F32)).astype(out.dtype)


VMEM = pl.BlockSpec(memory_space=pltpu.VMEM)


def shape(dims, kind):
    return jax.ShapeDtypeStruct(dims, kind)


def call(kernel, outs, scratch, n_in, name, flops, moved):
    held = sum(s.dtype.itemsize * functools.reduce(lambda x, y: x * y, s.shape) for s in outs + scratch)
    return pl.pallas_call(
        kernel,
        out_shape=outs,
        in_specs=[VMEM] * n_in,
        out_specs=[VMEM] * len(outs),
        scratch_shapes=[pltpu.VMEM(s.shape, s.dtype) for s in scratch],
        compiler_params=pltpu.CompilerParams(vmem_limit_bytes=min(held + 16 * MIB, 58 * MIB)),
        cost_estimate=pl.CostEstimate(flops=flops, bytes_accessed=moved, transcendentals=0),
        name=name,
    )


def exchange(x, axis, q):
    size = lax.axis_size(axis)
    return lax.ppermute(x, axis, [(i, i ^ q) for i in range(size)])


def shards(a_tiles, b_tiles, a_slots, b_slots):
    a_local = a_tiles.reshape(-1, FLAT)
    b_local = b_tiles.reshape(-1, FLAT)
    a_index = a_slots.reshape(1, -1)
    b_index = b_slots.reshape(1, -1)
    rows, cols, layers = lax.axis_size("row"), lax.axis_size("col"), lax.axis_size("layer")
    left_each, right_each = a_local.shape[0], b_local.shape[0]
    left_tiles = cols * left_each
    tiles = a_index.shape[1] // TASKS
    owned = tiles // layers
    pairs = right_each * left_tiles
    assert rows == 4 and layers == len(OWNER_ORDER)

    b_far = exchange(b_local, "row", 2)
    if cols == 2:
        a_parts = [a_local, exchange(a_local, "col", 1)]
    else:
        a_parts = [lax.all_gather(a_local, "col", axis=0, tiled=True)]
    (b_here,) = call(stage_kernel, [shape(b_local.shape, BF16)], [], 1, "stage", STAGE_FLOPS, MIB)(b_local)
    b_near = exchange(b_local, "row", 1)
    b_last = exchange(b_here, "row", 3)
    (sel,) = call(
        functools.partial(counts_kernel, cols == 2, left_tiles, left_each, right_each),
        [shape((tiles, rows * pairs), BF16)],
        [],
        2,
        "counts",
        2 * tiles * tiles * TASKS * TASKS,
        MIB,
    )(a_index, b_index)

    groups = (2,) if pairs * FLAT * 2 < 4 * MIB else (1, 1)
    raw = shape((right_each * LINES, LANES), F32)
    one = shape((LINES, pairs, LANES), BF16)
    shard_flops = 2 * pairs * LINES * LANES * LANES + 2 * pairs * tiles * FLAT
    acc, a_lines = call(
        functools.partial(own_kernel, groups, len(a_parts)),
        [shape((tiles, FLAT), F32), shape((left_tiles * LINES, LANES), BF16)],
        [raw, shape((LINES, max(groups) * pairs, LANES), BF16)],
        3 + len(a_parts),
        "own_and_near",
        2 * shard_flops,
        8 * MIB,
    )(sel, *a_parts, b_here, b_near)
    (acc,) = call(
        functools.partial(more_kernel, 2 * pairs),
        [shape((tiles, FLAT), F32)],
        [raw, one],
        4,
        "far_shard",
        shard_flops,
        4 * MIB,
    )(sel, a_lines, acc, b_far)
    own, far, cross, near = call(
        functools.partial(last_kernel, 3 * pairs),
        [shape((owned, FLAT), F32)] * 2 + [shape((owned, FLAT), BF16)] * 2,
        [raw, one],
        4,
        "last_shard",
        shard_flops,
        4 * MIB,
    )(sel, a_lines, acc, b_last)

    arrived_cross = exchange(cross, "layer", 1)
    arrived_near = exchange(near, "layer", 1)
    (joined,) = call(
        join_kernel, [shape((owned, FLAT), BF16)], [], 2, "join_cores", owned * FLAT, 1 * MIB
    )(far, arrived_cross)
    (out,) = call(
        add_kernel, [shape((owned, FLAT), BF16)], [], 3, "add_layers", 2 * owned * FLAT, 1 * MIB
    )(own, arrived_near, exchange(joined, "layer", 2))
    return out.reshape(1, 1, owned, FLAT)


def solution(mesh):
    in_specs = (
        P("row", "layer", "col", None, None),
        P("layer", "row", "col", None, None),
        P("row", "col", "layer", None),
        P("row", "col", "layer", None),
    )
    out_specs = P("row", "col", "layer", None)
    return jax.shard_map(shards, mesh=mesh, in_specs=in_specs, out_specs=out_specs, check_vma=False)
```

```python
import functools

import jax
import jax.numpy as jnp
from jax import lax
from jax.experimental import pallas as pl
from jax.experimental.pallas import tpu as pltpu
from jax.sharding import PartitionSpec as P

TILE = 64
TASKS = 8
FLAT = TILE * TILE
LANES = 128
LINES = FLAT // LANES
ROWS_AT_ONCE = 512
MIB = 1 << 20
STAGE_FLOPS = 2 * 10**9
F32, BF16 = jnp.float32, jnp.bfloat16
OWNER_ORDER = (0, 2, 3, 1)


def iota(shape, axis):
    return lax.broadcasted_iota(jnp.int32, shape, axis)


def split_inner_order():
    src, dst = iota((LANES, LANES), 0), iota((LANES, LANES), 1)
    half, rest = dst // TILE, dst % TILE
    wanted = half * TILE + 2 * (rest % (TILE // 2)) + rest // (TILE // 2)
    return jnp.where(src == wanted, 1.0, 0.0).astype(BF16)


def twice_on_diagonal(lines):
    low = iota(lines.shape, 1) < TILE
    turned = pltpu.roll(lines, TILE, 1)
    zero = jnp.zeros_like(lines)
    return jnp.concatenate(
        [
            jnp.where(low, lines, zero),
            jnp.where(low, turned, zero),
            jnp.where(low, zero, turned),
            jnp.where(low, zero, lines),
        ],
        axis=0,
    ).astype(BF16)


def loop(count, few, body):
    if count <= few:
        for i in range(count):
            body(i)
    else:
        pl.loop(0, count)(body)


def stage_kernel(b_ref, out):
    out[...] = b_ref[...]


def lower_kernel(b_ref, out):
    out[...] = b_ref[:out.shape[0], :]


def counts_kernel(swap, left_tiles, left_each, right_each, a_slots, b_slots, b_ref, sel, b_out, upper):
    b_out[...] = b_ref[...]
    upper[...] = b_ref[upper.shape[0]:, :]
    row, col, layer = lax.axis_index("row"), lax.axis_index("col"), lax.axis_index("layer")
    tiles, pairs = sel.shape
    tasks = tiles * TASKS
    owned = tiles // len(OWNER_ORDER)
    place = iota((tiles, tasks), 0)
    group = place // owned
    owner = jnp.zeros_like(group)
    for g, q in enumerate(OWNER_ORDER):
        owner = jnp.where(group == g, q, owner)
    tile = (owner ^ layer) * owned + place % owned
    mine = jnp.where(iota((tiles, tasks), 1) // TASKS == tile, 1.0, 0.0).astype(BF16)
    entry = iota((2 * TASKS, tasks), 0)
    at = iota((2 * TASKS, tasks), 1) % TASKS
    a_index, b_index = a_slots[...], b_slots[...]
    a_place = a_index ^ (col * left_each) if swap else a_index
    a_place = jnp.where(a_index < left_tiles, a_place, left_tiles)
    b_place = ((b_index // right_each) ^ row) * right_each + b_index % right_each
    spread = jnp.where(at == entry, a_place, 0) + jnp.where(at + TASKS == entry, b_place, 0)
    lists = lax.dot_general(
        mine, spread.astype(F32).astype(BF16), (((1,), (1,)), ((), ())), preferred_element_type=F32
    ).astype(jnp.int32)
    width = min(pairs, 1024)

    def some(part):
        here = iota((tiles, width), 1) + part * width
        total = jnp.zeros((tiles, width), F32)
        for e in range(TASKS):
            a_at, b_at = lists[:, e:e + 1], lists[:, TASKS + e:TASKS + e + 1]
            pair = jnp.where(a_at < left_tiles, b_at * left_tiles + a_at, -1)
            total = total + jnp.where(here == pair, 1.0, 0.0)
        sel[:, pl.ds(pl.multiple_of(part * width, width), width)] = total.astype(BF16)

    loop(pairs // width, 1, some)


def left_lines(a_refs, a_lines):
    order = split_inner_order()
    left_tiles = sum(r.shape[0] for r in a_refs)
    lines_at_once = min(LINES, max(1, ROWS_AT_ONCE // left_tiles))
    for i in range(0, LINES, lines_at_once):
        block = jnp.concatenate(
            [
                r[:, j * LANES:(j + 1) * LANES].astype(F32)
                for j in range(i, i + lines_at_once)
                for r in a_refs
            ],
            axis=0,
        ).astype(BF16)
        got = jnp.dot(block, order, preferred_element_type=F32)
        a_lines[i * left_tiles:(i + lines_at_once) * left_tiles, :] = got.astype(BF16)


def all_products(a_lines, b_ref, raw, prod, first):
    right_tiles = b_ref.shape[0]
    left_tiles = a_lines.shape[0] // LINES
    for i in range(LINES):
        raw[i * right_tiles:(i + 1) * right_tiles, :] = b_ref[:, i * LANES:(i + 1) * LANES].astype(F32)
    lines_at_once = min(LINES, max(1, ROWS_AT_ONCE // left_tiles))
    rows = lines_at_once * left_tiles

    def pair(p):
        right = jnp.concatenate(
            [twice_on_diagonal(raw[pl.ds(2 * p + h, LINES, stride=right_tiles), :]) for h in range(2)], axis=1
        )

        def some(part):
            at = part * rows if isinstance(part, int) else pl.multiple_of(part * rows, rows)
            got = jnp.dot(a_lines[pl.ds(at, rows), :], right, preferred_element_type=F32).astype(BF16)
            for j in range(lines_at_once):
                for h in range(2):
                    to = first + (2 * p + h) * left_tiles
                    to = to if isinstance(to, int) else pl.multiple_of(to, left_tiles)
                    prod[part * lines_at_once + j, pl.ds(to, left_tiles), :] = got[
                        j * left_tiles:(j + 1) * left_tiles, h * LANES:(h + 1) * LANES
                    ]

        loop(LINES // lines_at_once, 1, some)

    loop(right_tiles // 2, 8 if rows == a_lines.shape[0] else 1, pair)


def chosen_sums(sel, first, count, prod, put):
    for j in range(0, LINES, 2):
        right = jnp.concatenate([prod[j, :count, :], prod[j + 1, :count, :]], axis=1)
        put(
            slice(j * LANES, (j + 2) * LANES),
            jnp.dot(sel[:, first:first + count], right, preferred_element_type=F32),
        )


def first_kernel(groups, n_left, sel, *refs):
    shards = sum(groups)
    a_refs, b_refs = refs[:n_left], refs[n_left:n_left + shards]
    acc, a_lines, raw, prod = refs[n_left + shards:]
    left_lines(a_refs, a_lines)
    pairs = b_refs[0].shape[0] * a_lines.shape[0] // LINES
    shard = 0
    for count in groups:
        start = shard
        for i in range(count):
            all_products(a_lines, b_refs[shard], raw, prod, i * pairs)
            shard += 1

        def put(columns, value):
            acc[:, columns] = value if start == 0 else acc[:, columns] + value

        chosen_sums(sel, start * pairs, count * pairs, prod, put)


def last_kernel(start, n_parts, sel, a_lines, acc, *refs):
    b_refs, (own, far, cross, near, raw, prod) = refs[:n_parts], refs[n_parts:]
    each = a_lines.shape[0] // LINES
    owned = own.shape[0]
    done = 0
    for b_ref in b_refs:
        all_products(a_lines, b_ref, raw, prod, done)
        done += b_ref.shape[0] * each

    def put(columns, value):
        value = value + acc[:, columns]
        for i, out in enumerate((own, far, cross, near)):
            out[:, columns] = value[i * owned:(i + 1) * owned].astype(out.dtype)

    chosen_sums(sel, start, done, prod, put)


def join_kernel(far, arrived, out):
    out[...] = (far[...] + arrived[...].astype(F32)).astype(out.dtype)


def add_kernel(own, arrived, joined, out):
    out[...] = (own[...] + arrived[...].astype(F32) + joined[...].astype(F32)).astype(out.dtype)


VMEM = pl.BlockSpec(memory_space=pltpu.VMEM)


def shape(dims, kind):
    return jax.ShapeDtypeStruct(dims, kind)


def call(kernel, outs, scratch, n_in, name, flops, moved):
    held = sum(s.dtype.itemsize * functools.reduce(lambda x, y: x * y, s.shape) for s in outs + scratch)
    return pl.pallas_call(
        kernel,
        out_shape=outs,
        in_specs=[VMEM] * n_in,
        out_specs=[VMEM] * len(outs),
        scratch_shapes=[pltpu.VMEM(s.shape, s.dtype) for s in scratch],
        compiler_params=pltpu.CompilerParams(vmem_limit_bytes=min(held + 16 * MIB, 58 * MIB)),
        cost_estimate=pl.CostEstimate(flops=flops, bytes_accessed=moved, transcendentals=0),
        name=name,
    )


def exchange(x, axis, q):
    size = lax.axis_size(axis)
    return lax.ppermute(x, axis, [(i, i ^ q) for i in range(size)])


def shards(a_tiles, b_tiles, a_slots, b_slots):
    a_local = a_tiles.reshape(-1, FLAT)
    b_local = b_tiles.reshape(-1, FLAT)
    a_index = a_slots.reshape(1, -1)
    b_index = b_slots.reshape(1, -1)
    rows, cols, layers = lax.axis_size("row"), lax.axis_size("col"), lax.axis_size("layer")
    left_each, right_each = a_local.shape[0], b_local.shape[0]
    left_tiles = cols * left_each
    tiles = a_index.shape[1] // TASKS
    owned = tiles // layers
    pairs = right_each * left_tiles
    assert rows == 4 and layers == len(OWNER_ORDER)

    b_far = exchange(b_local, "row", 2)
    if cols == 2:
        a_parts = [a_local, exchange(a_local, "col", 1)]
    else:
        a_parts = [lax.all_gather(a_local, "col", axis=0, tiled=True)]
    upper = right_each // 2
    (b_staged,) = call(stage_kernel, [shape(b_local.shape, BF16)], [], 1, "stage", STAGE_FLOPS, MIB)(b_local)
    sel, b_here, b_upper = call(
        functools.partial(counts_kernel, cols == 2, left_tiles, left_each, right_each),
        [shape((tiles, rows * pairs), BF16), shape(b_local.shape, BF16), shape((upper, FLAT), BF16)],
        [],
        3,
        "counts",
        2 * tiles * tiles * TASKS * TASKS,
        MIB,
    )(a_index, b_index, b_staged)
    b_near = exchange(b_here, "row", 1)
    last_upper = exchange(b_upper, "row", 3)
    (b_lower,) = call(lower_kernel, [shape((right_each - upper, FLAT), BF16)], [], 1, "lower", upper * FLAT, MIB)(b_far)
    last_lower = exchange(b_lower, "row", 1)

    groups = (3,) if pairs * FLAT * 2 < 4 * MIB else (1, 1, 1)
    raw = shape((right_each * LINES, LANES), F32)
    half_raw = shape((upper * LINES, LANES), F32)
    shard_flops = 2 * pairs * LINES * LANES * LANES + 2 * pairs * tiles * FLAT
    acc, a_lines = call(
        functools.partial(first_kernel, groups, len(a_parts)),
        [shape((tiles, FLAT), F32), shape((left_tiles * LINES, LANES), BF16)],
        [raw, shape((LINES, max(groups) * pairs, LANES), BF16)],
        4 + len(a_parts),
        "own_and_near",
        3 * shard_flops,
        12 * MIB,
    )(sel, *a_parts, b_here, b_near, b_far)
    own, far, cross, near = call(
        functools.partial(last_kernel, 3 * pairs, 2),
        [shape((owned, FLAT), F32)] * 2 + [shape((owned, FLAT), BF16)] * 2,
        [half_raw, shape((LINES, pairs, LANES), BF16)],
        5,
        "last_shard",
        shard_flops,
        4 * MIB,
    )(sel, a_lines, acc, last_lower, last_upper)

    arrived_cross = exchange(cross, "layer", 1)
    arrived_near = exchange(near, "layer", 1)
    (joined,) = call(
        join_kernel, [shape((owned, FLAT), BF16)], [], 2, "join_cores", owned * FLAT, 1 * MIB
    )(far, arrived_cross)
    (out,) = call(
        add_kernel, [shape((owned, FLAT), BF16)], [], 3, "add_layers", 2 * owned * FLAT, 1 * MIB
    )(own, arrived_near, exchange(joined, "layer", 2))
    return out.reshape(1, 1, owned, FLAT)


def solution(mesh):
    in_specs = (
        P("row", "layer", "col", None, None),
        P("layer", "row", "col", None, None),
        P("row", "col", "layer", None),
        P("row", "col", "layer", None),
    )
    out_specs = P("row", "col", "layer", None)
    return jax.shard_map(shards, mesh=mesh, in_specs=in_specs, out_specs=out_specs, check_vma=False)
```

```python
import functools

import jax
import jax.numpy as jnp
from jax import lax
from jax.experimental import pallas as pl
from jax.experimental.pallas import tpu as pltpu
from jax.sharding import PartitionSpec as P

TILE = 64
TASKS = 8
FLAT = TILE * TILE
LANES = 128
LINES = FLAT // LANES
ROWS_AT_ONCE = 512
TILES_AT_ONCE = 4
LINES_AT_ONCE = 4
MIB = 1 << 20
STAGE_FLOPS = 2 * 10**9
F32, BF16 = jnp.float32, jnp.bfloat16
OWNER_ORDER = (0, 2, 3, 1)


def iota(shape, axis):
    return lax.broadcasted_iota(jnp.int32, shape, axis)


def ones_where(hit):
    return jnp.where(hit, 1.0, 0.0).astype(BF16)


def split_inner_order():
    src, dst = iota((LANES, LANES), 0), iota((LANES, LANES), 1)
    half, rest = dst // TILE, dst % TILE
    wanted = half * TILE + 2 * (rest % (TILE // 2)) + rest // (TILE // 2)
    return ones_where(src == wanted)


def twice_on_diagonal(lines):
    low = ones_where(iota(lines.shape, 1) < TILE)
    high = ones_where(iota(lines.shape, 1) >= TILE)
    turned = pltpu.roll(lines, TILE, 1).astype(BF16)
    lines = lines.astype(BF16)
    return jnp.concatenate([lines * low, turned * low, turned * high, lines * high], axis=0)


def loop(count, few, body):
    if count <= few:
        for i in range(count):
            body(i)
    else:
        pl.loop(0, count)(body)


def stage_kernel(*refs):
    for ref, out in zip(refs[:len(refs) // 2], refs[len(refs) // 2:]):
        out[...] = ref[...]


def counts_kernel(swap, left_tiles, left_each, right_each, a_slots, b_slots, sel):
    row, col, layer = lax.axis_index("row"), lax.axis_index("col"), lax.axis_index("layer")
    tiles, pairs = sel.shape
    tasks = tiles * TASKS
    owned = tiles // len(OWNER_ORDER)
    place = iota((tiles, tasks), 0)
    group = place // owned
    owner = jnp.zeros_like(group)
    for g, q in enumerate(OWNER_ORDER):
        owner = jnp.where(group == g, q, owner)
    tile = (owner ^ layer) * owned + place % owned
    mine = jnp.where(iota((tiles, tasks), 1) // TASKS == tile, 1.0, 0.0).astype(BF16)
    entry = iota((2 * TASKS, tasks), 0)
    at = iota((2 * TASKS, tasks), 1) % TASKS
    a_index, b_index = a_slots[...], b_slots[...]
    a_place = a_index ^ (col * left_each) if swap else a_index
    a_place = jnp.where(a_index < left_tiles, a_place, left_tiles)
    b_place = ((b_index // right_each) ^ row) * right_each + b_index % right_each
    spread = jnp.where(at == entry, a_place, 0) + jnp.where(at + TASKS == entry, b_place, 0)
    lists = lax.dot_general(
        mine, spread.astype(F32).astype(BF16), (((1,), (1,)), ((), ())), preferred_element_type=F32
    ).astype(jnp.int32)
    width = min(pairs, 1024)

    def some(part):
        here = iota((tiles, width), 1) + part * width
        total = jnp.zeros((tiles, width), F32)
        for e in range(TASKS):
            a_at, b_at = lists[:, e:e + 1], lists[:, TASKS + e:TASKS + e + 1]
            pair = jnp.where(a_at < left_tiles, b_at * left_tiles + a_at, -1)
            total = total + jnp.where(here == pair, 1.0, 0.0)
        sel[:, pl.ds(pl.multiple_of(part * width, width), width)] = total.astype(BF16)

    loop(pairs // width, 1, some)


def left_lines(a_refs, a_lines):
    order = split_inner_order()
    left_tiles = sum(r.shape[0] for r in a_refs)
    lines_at_once = min(LINES, max(1, ROWS_AT_ONCE // left_tiles))
    for i in range(0, LINES, lines_at_once):
        block = jnp.concatenate(
            [
                r[:, j * LANES:(j + 1) * LANES].astype(F32)
                for j in range(i, i + lines_at_once)
                for r in a_refs
            ],
            axis=0,
        ).astype(BF16)
        got = jnp.dot(block, order, preferred_element_type=F32)
        a_lines[i * left_tiles:(i + lines_at_once) * left_tiles, :] = got.astype(BF16)


def all_products(a_lines, b_ref, raw, prod, first):
    right_tiles = b_ref.shape[0]
    left_tiles = a_lines.shape[0] // LINES
    for i in range(LINES):
        raw[i * right_tiles:(i + 1) * right_tiles, :] = b_ref[:, i * LANES:(i + 1) * LANES].astype(F32)
    lines_at_once = min(LINES, max(1, ROWS_AT_ONCE // left_tiles))
    rows = lines_at_once * left_tiles

    def some_tiles(p):
        right = jnp.concatenate(
            [
                twice_on_diagonal(raw[pl.ds(p * TILES_AT_ONCE + h, LINES, stride=right_tiles), :])
                for h in range(TILES_AT_ONCE)
            ],
            axis=1,
        )

        def some(part):
            at = part * rows if isinstance(part, int) else pl.multiple_of(part * rows, rows)
            got = jnp.dot(a_lines[pl.ds(at, rows), :], right, preferred_element_type=F32).astype(BF16)
            for j in range(lines_at_once):
                for h in range(TILES_AT_ONCE):
                    to = first + (p * TILES_AT_ONCE + h) * left_tiles
                    to = to if isinstance(to, int) else pl.multiple_of(to, left_tiles)
                    prod[part * lines_at_once + j, pl.ds(to, left_tiles), :] = got[
                        j * left_tiles:(j + 1) * left_tiles, h * LANES:(h + 1) * LANES
                    ]

        loop(LINES // lines_at_once, 1, some)

    loop(right_tiles // TILES_AT_ONCE, 8 if rows == a_lines.shape[0] else 1, some_tiles)


def chosen_sums(sel, first, count, prod, put):
    for j in range(0, LINES, LINES_AT_ONCE):
        right = jnp.concatenate([prod[j + i, :count, :] for i in range(LINES_AT_ONCE)], axis=1)
        put(
            slice(j * LANES, (j + LINES_AT_ONCE) * LANES),
            jnp.dot(sel[:, first:first + count], right, preferred_element_type=F32),
        )


def own_kernel(groups, n_left, sel, *refs):
    shards = sum(groups)
    a_refs, b_refs = refs[:n_left], refs[n_left:n_left + shards]
    acc, a_lines, raw, prod = refs[n_left + shards:]
    left_lines(a_refs, a_lines)
    add_shards(0, groups, sel, a_lines, b_refs, None, acc, raw, prod)


def more_kernel(start, sel, a_lines, acc, b_ref, out, raw, prod):
    add_shards(start, (1,), sel, a_lines, (b_ref,), acc, out, raw, prod)


def add_shards(start, groups, sel, a_lines, b_refs, acc, out, raw, prod):
    each = a_lines.shape[0] // LINES
    taken = 0
    for count in groups:
        done = 0
        before = out if taken else acc
        for b_ref in b_refs[taken:taken + count]:
            all_products(a_lines, b_ref, raw, prod, done)
            done += b_ref.shape[0] * each

        def put(columns, value):
            out[:, columns] = value if before is None else value + before[:, columns]

        chosen_sums(sel, start, done, prod, put)
        taken += count
        start += done


def last_kernel(start, sel, a_lines, acc, b_ref, own, far, cross, near, raw, prod):
    pairs = b_ref.shape[0] * a_lines.shape[0] // LINES
    owned = own.shape[0]
    all_products(a_lines, b_ref, raw, prod, 0)

    def put(columns, value):
        value = value + acc[:, columns]
        for i, out in enumerate((own, far, cross, near)):
            out[:, columns] = value[i * owned:(i + 1) * owned].astype(out.dtype)

    chosen_sums(sel, start, pairs, prod, put)


def join_kernel(far, arrived, out):
    out[...] = (far[...] + arrived[...].astype(F32)).astype(out.dtype)


def add_kernel(own, arrived, joined, out):
    out[...] = (own[...] + arrived[...].astype(F32) + joined[...].astype(F32)).astype(out.dtype)


VMEM = pl.BlockSpec(memory_space=pltpu.VMEM)


def shape(dims, kind):
    return jax.ShapeDtypeStruct(dims, kind)


def call(kernel, outs, scratch, n_in, name, flops, moved):
    held = sum(s.dtype.itemsize * functools.reduce(lambda x, y: x * y, s.shape) for s in outs + scratch)
    return pl.pallas_call(
        kernel,
        out_shape=outs,
        in_specs=[VMEM] * n_in,
        out_specs=[VMEM] * len(outs),
        scratch_shapes=[pltpu.VMEM(s.shape, s.dtype) for s in scratch],
        compiler_params=pltpu.CompilerParams(vmem_limit_bytes=min(held + 16 * MIB, 58 * MIB)),
        cost_estimate=pl.CostEstimate(flops=flops, bytes_accessed=moved, transcendentals=0),
        name=name,
    )


def exchange(x, axis, q):
    size = lax.axis_size(axis)
    return lax.ppermute(x, axis, [(i, i ^ q) for i in range(size)])


def shards(a_tiles, b_tiles, a_slots, b_slots):
    a_local = a_tiles.reshape(-1, FLAT)
    b_local = b_tiles.reshape(-1, FLAT)
    a_index = a_slots.reshape(1, -1)
    b_index = b_slots.reshape(1, -1)
    rows, cols, layers = lax.axis_size("row"), lax.axis_size("col"), lax.axis_size("layer")
    left_each, right_each = a_local.shape[0], b_local.shape[0]
    left_tiles = cols * left_each
    tiles = a_index.shape[1] // TASKS
    owned = tiles // layers
    pairs = right_each * left_tiles
    assert rows == 4 and layers == len(OWNER_ORDER)

    b_far = exchange(b_local, "row", 2)
    if cols == 2:
        a_parts = [a_local, exchange(a_local, "col", 1)]
    else:
        a_parts = [lax.all_gather(a_local, "col", axis=0, tiled=True)]
    (b_here,) = call(stage_kernel, [shape(b_local.shape, BF16)], [], 1, "stage", STAGE_FLOPS, MIB)(b_local)
    b_near = exchange(b_local, "row", 1)
    b_last = exchange(b_here, "row", 3)
    (sel,) = call(
        functools.partial(counts_kernel, cols == 2, left_tiles, left_each, right_each),
        [shape((tiles, rows * pairs), BF16)],
        [],
        2,
        "counts",
        2 * tiles * tiles * TASKS * TASKS,
        MIB,
    )(a_index, b_index)

    groups = (2,) if pairs * FLAT * 2 < 4 * MIB else (1, 1)
    raw = shape((right_each * LINES, LANES), F32)
    one = shape((LINES, pairs, LANES), BF16)
    shard_flops = 2 * pairs * LINES * LANES * LANES + 2 * pairs * tiles * FLAT
    acc, a_lines = call(
        functools.partial(own_kernel, groups, len(a_parts)),
        [shape((tiles, FLAT), F32), shape((left_tiles * LINES, LANES), BF16)],
        [raw, shape((LINES, max(groups) * pairs, LANES), BF16)],
        3 + len(a_parts),
        "own_and_near",
        2 * shard_flops,
        8 * MIB,
    )(sel, *a_parts, b_here, b_near)
    (acc,) = call(
        functools.partial(more_kernel, 2 * pairs),
        [shape((tiles, FLAT), F32)],
        [raw, one],
        4,
        "far_shard",
        shard_flops,
        4 * MIB,
    )(sel, a_lines, acc, b_far)
    own, far, cross, near = call(
        functools.partial(last_kernel, 3 * pairs),
        [shape((owned, FLAT), F32)] * 2 + [shape((owned, FLAT), BF16)] * 2,
        [raw, one],
        4,
        "last_shard",
        shard_flops,
        4 * MIB,
    )(sel, a_lines, acc, b_last)

    arrived_cross = exchange(cross, "layer", 1)
    arrived_near = exchange(near, "layer", 1)
    (joined,) = call(
        join_kernel, [shape((owned, FLAT), BF16)], [], 2, "join_cores", owned * FLAT, 1 * MIB
    )(far, arrived_cross)
    (out,) = call(
        add_kernel, [shape((owned, FLAT), BF16)], [], 3, "add_layers", 2 * owned * FLAT, 1 * MIB
    )(own, arrived_near, exchange(joined, "layer", 2))
    return out.reshape(1, 1, owned, FLAT)


def solution(mesh):
    in_specs = (
        P("row", "layer", "col", None, None),
        P("layer", "row", "col", None, None),
        P("row", "col", "layer", None),
        P("row", "col", "layer", None),
    )
    out_specs = P("row", "col", "layer", None)
    return jax.shard_map(shards, mesh=mesh, in_specs=in_specs, out_specs=out_specs, check_vma=False)
```

```python
import functools

import jax
import jax.numpy as jnp
from jax import lax
from jax.experimental import pallas as pl
from jax.experimental.pallas import tpu as pltpu
from jax.sharding import PartitionSpec as P

TILE = 64
TASKS = 8
FLAT = TILE * TILE
LANES = 128
LINES = FLAT // LANES
ROWS_AT_ONCE = 512
TILES_AT_ONCE = 4
LINES_AT_ONCE = 4
MIB = 1 << 20
OWN_FLOPS = 500 * 10**6
STAGE_FLOPS = 2 * 10**9
F32, BF16 = jnp.float32, jnp.bfloat16
OWNER_ORDER = (0, 2, 3, 1)


def iota(shape, axis):
    return lax.broadcasted_iota(jnp.int32, shape, axis)


def ones_where(hit):
    return jnp.where(hit, 1.0, 0.0).astype(BF16)


def split_inner_order():
    src, dst = iota((LANES, LANES), 0), iota((LANES, LANES), 1)
    half, rest = dst // TILE, dst % TILE
    wanted = half * TILE + 2 * (rest % (TILE // 2)) + rest // (TILE // 2)
    return ones_where(src == wanted)


def twice_on_diagonal(lines):
    low = ones_where(iota(lines.shape, 1) < TILE)
    high = ones_where(iota(lines.shape, 1) >= TILE)
    turned = pltpu.roll(lines, TILE, 1).astype(BF16)
    lines = lines.astype(BF16)
    return jnp.concatenate([lines * low, turned * low, turned * high, lines * high], axis=0)


def loop(count, few, body):
    if count <= few:
        for i in range(count):
            body(i)
    else:
        pl.loop(0, count)(body)


def stage_kernel(b_ref, out, straight):
    out[...] = b_ref[...]
    straight[...] = b_ref[:, b_ref.shape[1] - straight.shape[1]:]


def first_columns_kernel(b_ref, out):
    out[...] = b_ref[:, :out.shape[1]]


def counts_kernel(swap, left_tiles, left_each, right_each, a_slots, b_slots, sel):
    row, col, layer = lax.axis_index("row"), lax.axis_index("col"), lax.axis_index("layer")
    tiles, pairs = sel.shape
    tasks = tiles * TASKS
    owned = tiles // len(OWNER_ORDER)
    place = iota((tiles, tasks), 0)
    group = place // owned
    owner = jnp.zeros_like(group)
    for g, q in enumerate(OWNER_ORDER):
        owner = jnp.where(group == g, q, owner)
    tile = (owner ^ layer) * owned + place % owned
    mine = jnp.where(iota((tiles, tasks), 1) // TASKS == tile, 1.0, 0.0).astype(BF16)
    entry = iota((2 * TASKS, tasks), 0)
    at = iota((2 * TASKS, tasks), 1) % TASKS
    a_index, b_index = a_slots[...], b_slots[...]
    a_place = a_index ^ (col * left_each) if swap else a_index
    a_place = jnp.where(a_index < left_tiles, a_place, left_tiles)
    b_place = ((b_index // right_each) ^ row) * right_each + b_index % right_each
    spread = jnp.where(at == entry, a_place, 0) + jnp.where(at + TASKS == entry, b_place, 0)
    lists = lax.dot_general(
        mine, spread.astype(F32).astype(BF16), (((1,), (1,)), ((), ())), preferred_element_type=F32
    ).astype(jnp.int32)
    width = min(pairs, 1024)

    def some(part):
        here = iota((tiles, width), 1) + part * width
        total = jnp.zeros((tiles, width), F32)
        for e in range(TASKS):
            a_at, b_at = lists[:, e:e + 1], lists[:, TASKS + e:TASKS + e + 1]
            pair = jnp.where(a_at < left_tiles, b_at * left_tiles + a_at, -1)
            total = total + jnp.where(here == pair, 1.0, 0.0)
        sel[:, pl.ds(pl.multiple_of(part * width, width), width)] = total.astype(BF16)

    loop(pairs // width, 1, some)


def left_lines(a_refs, a_lines):
    order = split_inner_order()
    left_tiles = sum(r.shape[0] for r in a_refs)
    lines_at_once = min(LINES, max(1, ROWS_AT_ONCE // left_tiles))
    for i in range(0, LINES, lines_at_once):
        block = jnp.concatenate(
            [
                r[:, j * LANES:(j + 1) * LANES].astype(F32)
                for j in range(i, i + lines_at_once)
                for r in a_refs
            ],
            axis=0,
        ).astype(BF16)
        got = jnp.dot(block, order, preferred_element_type=F32)
        a_lines[i * left_tiles:(i + lines_at_once) * left_tiles, :] = got.astype(BF16)


def all_products(a_lines, b_refs, raw, prod, first):
    right_tiles = b_refs[0].shape[0]
    left_tiles = a_lines.shape[0] // LINES
    blocks = [(b_ref, i) for b_ref in b_refs for i in range(0, b_ref.shape[1], LANES)]
    for line, (b_ref, i) in enumerate(blocks):
        raw[line * right_tiles:(line + 1) * right_tiles, :] = b_ref[:, i:i + LANES].astype(F32)
    lines_at_once = min(LINES, max(1, ROWS_AT_ONCE // left_tiles))
    rows = lines_at_once * left_tiles

    def some_tiles(p):
        right = jnp.concatenate(
            [
                twice_on_diagonal(raw[pl.ds(p * TILES_AT_ONCE + h, LINES, stride=right_tiles), :])
                for h in range(TILES_AT_ONCE)
            ],
            axis=1,
        )

        def some(part):
            at = part * rows if isinstance(part, int) else pl.multiple_of(part * rows, rows)
            got = jnp.dot(a_lines[pl.ds(at, rows), :], right, preferred_element_type=F32).astype(BF16)
            for j in range(lines_at_once):
                for h in range(TILES_AT_ONCE):
                    to = first + (p * TILES_AT_ONCE + h) * left_tiles
                    to = to if isinstance(to, int) else pl.multiple_of(to, left_tiles)
                    prod[part * lines_at_once + j, pl.ds(to, left_tiles), :] = got[
                        j * left_tiles:(j + 1) * left_tiles, h * LANES:(h + 1) * LANES
                    ]

        loop(LINES // lines_at_once, 1, some)

    loop(right_tiles // TILES_AT_ONCE, 8 if rows == a_lines.shape[0] else 1, some_tiles)


def chosen_sums(sel, first, count, prod, put):
    for j in range(0, LINES, LINES_AT_ONCE):
        right = jnp.concatenate([prod[j + i, :count, :] for i in range(LINES_AT_ONCE)], axis=1)
        put(
            slice(j * LANES, (j + LINES_AT_ONCE) * LANES),
            jnp.dot(sel[:, first:first + count], right, preferred_element_type=F32),
        )


def own_kernel(groups, n_left, sel, *refs):
    shards = sum(groups)
    a_refs, b_refs = refs[:n_left], refs[n_left:n_left + shards]
    acc, a_lines, raw, prod = refs[n_left + shards:]
    left_lines(a_refs, a_lines)
    add_shards(0, groups, sel, a_lines, b_refs, None, acc, raw, prod)


def more_kernel(start, groups, sel, a_lines, acc, *refs):
    b_refs, (out, raw, prod) = refs[:-3], refs[-3:]
    add_shards(start, groups, sel, a_lines, b_refs, acc, out, raw, prod)


def add_shards(start, groups, sel, a_lines, b_refs, acc, out, raw, prod):
    each = a_lines.shape[0] // LINES
    taken = 0
    for count in groups:
        done = 0
        before = out if taken else acc
        for b_ref in b_refs[taken:taken + count]:
            all_products(a_lines, [b_ref], raw, prod, done)
            done += b_ref.shape[0] * each

        def put(columns, value):
            out[:, columns] = value if before is None else value + before[:, columns]

        chosen_sums(sel, start, done, prod, put)
        taken += count
        start += done


def last_kernel(start, sel, a_lines, acc, b_sent_on, b_straight, own, far, cross, near, raw, prod):
    pairs = b_straight.shape[0] * a_lines.shape[0] // LINES
    owned = own.shape[0]
    all_products(a_lines, [b_sent_on, b_straight], raw, prod, 0)

    def put(columns, value):
        value = value + acc[:, columns]
        for i, out in enumerate((own, far, cross, near)):
            out[:, columns] = value[i * owned:(i + 1) * owned].astype(out.dtype)

    chosen_sums(sel, start, pairs, prod, put)


def join_kernel(far, arrived, out):
    out[...] = (far[...] + arrived[...].astype(F32)).astype(out.dtype)


def add_kernel(own, arrived, joined, out):
    out[...] = (own[...] + arrived[...].astype(F32) + joined[...].astype(F32)).astype(out.dtype)


VMEM = pl.BlockSpec(memory_space=pltpu.VMEM)


def shape(dims, kind):
    return jax.ShapeDtypeStruct(dims, kind)


def call(kernel, outs, scratch, n_in, name, flops, moved):
    held = sum(s.dtype.itemsize * functools.reduce(lambda x, y: x * y, s.shape) for s in outs + scratch)
    return pl.pallas_call(
        kernel,
        out_shape=outs,
        in_specs=[VMEM] * n_in,
        out_specs=[VMEM] * len(outs),
        scratch_shapes=[pltpu.VMEM(s.shape, s.dtype) for s in scratch],
        compiler_params=pltpu.CompilerParams(vmem_limit_bytes=min(held + 16 * MIB, 58 * MIB)),
        cost_estimate=pl.CostEstimate(flops=flops, bytes_accessed=moved, transcendentals=0),
        name=name,
    )


def exchange(x, axis, q):
    size = lax.axis_size(axis)
    return lax.ppermute(x, axis, [(i, i ^ q) for i in range(size)])


def shards(a_tiles, b_tiles, a_slots, b_slots):
    a_local = a_tiles.reshape(-1, FLAT)
    b_local = b_tiles.reshape(-1, FLAT)
    a_index = a_slots.reshape(1, -1)
    b_index = b_slots.reshape(1, -1)
    rows, cols, layers = lax.axis_size("row"), lax.axis_size("col"), lax.axis_size("layer")
    left_each, right_each = a_local.shape[0], b_local.shape[0]
    left_tiles = cols * left_each
    tiles = a_index.shape[1] // TASKS
    owned = tiles // layers
    pairs = right_each * left_tiles
    assert rows == 4 and layers == len(OWNER_ORDER)

    b_far = exchange(b_local, "row", 2)
    if cols == 2:
        a_parts = [a_local, exchange(a_local, "col", 1)]
    else:
        a_parts = [lax.all_gather(a_local, "col", axis=0, tiled=True)]
    sent_on = FLAT // 4
    b_here, b_straight = call(
        stage_kernel,
        [shape(b_local.shape, BF16), shape((right_each, FLAT - sent_on), BF16)],
        [],
        1,
        "stage",
        STAGE_FLOPS,
        MIB,
    )(b_local)
    b_near = exchange(b_local, "row", 1)
    last_straight = exchange(b_straight, "row", 3)
    (b_first,) = call(
        first_columns_kernel, [shape((right_each, sent_on), BF16)], [], 1, "first_columns", FLAT, MIB
    )(b_far)
    last_sent_on = exchange(b_first, "row", 1)
    (sel,) = call(
        functools.partial(counts_kernel, cols == 2, left_tiles, left_each, right_each),
        [shape((tiles, rows * pairs), BF16)],
        [],
        2,
        "counts",
        2 * tiles * tiles * TASKS * TASKS,
        MIB,
    )(a_index, b_index)

    groups = (2,) if pairs * FLAT * 2 < 4 * MIB else (1, 1)
    raw = shape((right_each * LINES, LANES), F32)
    one = shape((LINES, pairs, LANES), BF16)
    shard_flops = 2 * pairs * LINES * LANES * LANES + 2 * pairs * tiles * FLAT
    acc, a_lines = call(
        functools.partial(own_kernel, (1,), len(a_parts)),
        [shape((tiles, FLAT), F32), shape((left_tiles * LINES, LANES), BF16)],
        [raw, one],
        2 + len(a_parts),
        "own_shard",
        OWN_FLOPS,
        4 * MIB,
    )(sel, *a_parts, b_here)
    (acc,) = call(
        functools.partial(more_kernel, pairs, groups),
        [shape((tiles, FLAT), F32)],
        [raw, shape((LINES, max(groups) * pairs, LANES), BF16)],
        5,
        "near_and_far",
        2 * shard_flops,
        8 * MIB,
    )(sel, a_lines, acc, b_near, b_far)
    own, far, cross, near = call(
        functools.partial(last_kernel, 3 * pairs),
        [shape((owned, FLAT), F32)] * 2 + [shape((owned, FLAT), BF16)] * 2,
        [raw, one],
        5,
        "last_shard",
        shard_flops,
        4 * MIB,
    )(sel, a_lines, acc, last_sent_on, last_straight)

    arrived_cross = exchange(cross, "layer", 1)
    arrived_near = exchange(near, "layer", 1)
    (joined,) = call(
        join_kernel, [shape((owned, FLAT), BF16)], [], 2, "join_cores", owned * FLAT, 1 * MIB
    )(far, arrived_cross)
    (out,) = call(
        add_kernel, [shape((owned, FLAT), BF16)], [], 3, "add_layers", 2 * owned * FLAT, 1 * MIB
    )(own, arrived_near, exchange(joined, "layer", 2))
    return out.reshape(1, 1, owned, FLAT)


def solution(mesh):
    in_specs = (
        P("row", "layer", "col", None, None),
        P("layer", "row", "col", None, None),
        P("row", "col", "layer", None),
        P("row", "col", "layer", None),
    )
    out_specs = P("row", "col", "layer", None)
    return jax.shard_map(shards, mesh=mesh, in_specs=in_specs, out_specs=out_specs, check_vma=False)
```

```python
import functools

import jax
import jax.numpy as jnp
from jax import lax
from jax.experimental import pallas as pl
from jax.experimental.pallas import tpu as pltpu
from jax.sharding import PartitionSpec as P

TILE = 64
TASKS = 8
FLAT = TILE * TILE
LANES = 128
LINES = FLAT // LANES
ROWS_AT_ONCE = 512
TILES_AT_ONCE = 4
LINES_AT_ONCE = 4
MIB = 1 << 20
STAGE_FLOPS = 2 * 10**9
F32, BF16 = jnp.float32, jnp.bfloat16
OWNER_ORDER = (0, 2, 3, 1)


def iota(shape, axis):
    return lax.broadcasted_iota(jnp.int32, shape, axis)


def ones_where(hit):
    return jnp.where(hit, 1.0, 0.0).astype(BF16)


def split_inner_order():
    src, dst = iota((LANES, LANES), 0), iota((LANES, LANES), 1)
    half, rest = dst // TILE, dst % TILE
    wanted = half * TILE + 2 * (rest % (TILE // 2)) + rest // (TILE // 2)
    return ones_where(src == wanted)


def twice_on_diagonal(lines):
    low = ones_where(iota(lines.shape, 1) < TILE)
    high = ones_where(iota(lines.shape, 1) >= TILE)
    turned = pltpu.roll(lines, TILE, 1).astype(BF16)
    lines = lines.astype(BF16)
    return jnp.concatenate([lines * low, turned * low, turned * high, lines * high], axis=0)


def loop(count, few, body):
    if count <= few:
        for i in range(count):
            body(i)
    else:
        pl.loop(0, count)(body)


def stage_kernel(*refs):
    for ref, out in zip(refs[:len(refs) // 2], refs[len(refs) // 2:]):
        out[...] = ref[...]


def counts_kernel(swap, left_tiles, left_each, right_each, a_slots, b_slots, sel):
    row, col, layer = lax.axis_index("row"), lax.axis_index("col"), lax.axis_index("layer")
    tiles, pairs = sel.shape
    tasks = tiles * TASKS
    owned = tiles // len(OWNER_ORDER)
    place = iota((tiles, tasks), 0)
    group = place // owned
    owner = jnp.zeros_like(group)
    for g, q in enumerate(OWNER_ORDER):
        owner = jnp.where(group == g, q, owner)
    tile = (owner ^ layer) * owned + place % owned
    mine = jnp.where(iota((tiles, tasks), 1) // TASKS == tile, 1.0, 0.0).astype(BF16)
    entry = iota((2 * TASKS, tasks), 0)
    at = iota((2 * TASKS, tasks), 1) % TASKS
    a_index, b_index = a_slots[...], b_slots[...]
    a_place = a_index ^ (col * left_each) if swap else a_index
    a_place = jnp.where(a_index < left_tiles, a_place, left_tiles)
    b_place = ((b_index // right_each) ^ row) * right_each + b_index % right_each
    spread = jnp.where(at == entry, a_place, 0) + jnp.where(at + TASKS == entry, b_place, 0)
    lists = lax.dot_general(
        mine, spread.astype(F32).astype(BF16), (((1,), (1,)), ((), ())), preferred_element_type=F32
    ).astype(jnp.int32)
    width = min(pairs, 1024)

    def some(part):
        here = iota((tiles, width), 1) + part * width
        total = jnp.zeros((tiles, width), F32)
        for e in range(TASKS):
            a_at, b_at = lists[:, e:e + 1], lists[:, TASKS + e:TASKS + e + 1]
            pair = jnp.where(a_at < left_tiles, b_at * left_tiles + a_at, -1)
            total = total + jnp.where(here == pair, 1.0, 0.0)
        sel[:, pl.ds(pl.multiple_of(part * width, width), width)] = total.astype(BF16)

    loop(pairs // width, 1, some)


def left_lines(a_refs, a_lines):
    order = split_inner_order()
    left_tiles = sum(r.shape[0] for r in a_refs)
    lines_at_once = min(LINES, max(1, ROWS_AT_ONCE // left_tiles))
    for i in range(0, LINES, lines_at_once):
        block = jnp.concatenate(
            [
                r[:, j * LANES:(j + 1) * LANES].astype(F32)
                for j in range(i, i + lines_at_once)
                for r in a_refs
            ],
            axis=0,
        ).astype(BF16)
        got = jnp.dot(block, order, preferred_element_type=F32)
        a_lines[i * left_tiles:(i + lines_at_once) * left_tiles, :] = got.astype(BF16)


def all_products(a_lines, b_ref, raw, prod, first, first_line=0):
    right_tiles = b_ref.shape[0]
    left_tiles = a_lines.shape[0] // LINES
    for i in range(LINES):
        raw[i * right_tiles:(i + 1) * right_tiles, :] = b_ref[:, i * LANES:(i + 1) * LANES].astype(F32)
    lines = prod.shape[0]
    lines_at_once = min(lines, max(1, ROWS_AT_ONCE // left_tiles))
    rows = lines_at_once * left_tiles

    def some_tiles(p):
        right = jnp.concatenate(
            [
                twice_on_diagonal(raw[pl.ds(p * TILES_AT_ONCE + h, LINES, stride=right_tiles), :])
                for h in range(TILES_AT_ONCE)
            ],
            axis=1,
        )

        def some(part):
            at = first_line * left_tiles + part * rows
            at = at if isinstance(at, int) else pl.multiple_of(at, rows)
            got = jnp.dot(a_lines[pl.ds(at, rows), :], right, preferred_element_type=F32).astype(BF16)
            for j in range(lines_at_once):
                for h in range(TILES_AT_ONCE):
                    to = first + (p * TILES_AT_ONCE + h) * left_tiles
                    to = to if isinstance(to, int) else pl.multiple_of(to, left_tiles)
                    prod[part * lines_at_once + j, pl.ds(to, left_tiles), :] = got[
                        j * left_tiles:(j + 1) * left_tiles, h * LANES:(h + 1) * LANES
                    ]

        loop(lines // lines_at_once, 1, some)

    loop(right_tiles // TILES_AT_ONCE, 8 if lines == lines_at_once else 1, some_tiles)


def chosen_sums(sel, first, count, prod, put):
    for j in range(0, prod.shape[0], LINES_AT_ONCE):
        right = jnp.concatenate([prod[j + i, :count, :] for i in range(LINES_AT_ONCE)], axis=1)
        put(
            slice(j * LANES, (j + LINES_AT_ONCE) * LANES),
            jnp.dot(sel[:, first:first + count], right, preferred_element_type=F32),
        )


def own_kernel(groups, n_left, sel, *refs):
    shards = sum(groups)
    a_refs, b_refs = refs[:n_left], refs[n_left:n_left + shards]
    acc, a_lines, raw, prod = refs[n_left + shards:]
    left_lines(a_refs, a_lines)
    add_shards(0, groups, sel, a_lines, b_refs, None, acc, raw, prod)


def more_kernel(start, sel, a_lines, acc, b_ref, out, raw, prod):
    add_shards(start, (1,), sel, a_lines, (b_ref,), acc, out, raw, prod)


def add_shards(start, groups, sel, a_lines, b_refs, acc, out, raw, prod):
    each = a_lines.shape[0] // LINES
    taken = 0
    for count in groups:
        done = 0
        before = out if taken else acc
        for b_ref in b_refs[taken:taken + count]:
            all_products(a_lines, b_ref, raw, prod, done)
            done += b_ref.shape[0] * each

        def put(columns, value):
            out[:, columns] = value if before is None else value + before[:, columns]

        chosen_sums(sel, start, done, prod, put)
        taken += count
        start += done


def last_kernel(start, first_line, sel, a_lines, acc, b_ref, own, far, sent, raw, prod):
    pairs = b_ref.shape[0] * a_lines.shape[0] // LINES
    owned = own.shape[0]
    all_products(a_lines, b_ref, raw, prod, 0, first_line)

    def put(columns, value):
        value = value + acc[:, first_line * LANES + columns.start:first_line * LANES + columns.stop]
        own[:, columns] = value[:owned]
        far[:, columns] = value[owned:2 * owned]
        sent[:, columns] = value[2 * owned:].astype(sent.dtype)

    chosen_sums(sel, start, pairs, prod, put)


def join_kernel(far, arrived, out):
    out[...] = (far[...] + arrived[:out.shape[0], :].astype(F32)).astype(out.dtype)


def add_kernel(*refs):
    out = refs[-1]
    count, done = out.shape[0], 0
    for own, arrived, joined in zip(refs[0:-1:3], refs[1:-1:3], refs[2:-1:3]):
        total = own[...] + arrived[count:, :].astype(F32) + joined[...].astype(F32)
        out[:, done:done + total.shape[1]] = total.astype(out.dtype)
        done += total.shape[1]


VMEM = pl.BlockSpec(memory_space=pltpu.VMEM)


def shape(dims, kind):
    return jax.ShapeDtypeStruct(dims, kind)


def call(kernel, outs, scratch, n_in, name, flops, moved):
    held = sum(s.dtype.itemsize * functools.reduce(lambda x, y: x * y, s.shape) for s in outs + scratch)
    return pl.pallas_call(
        kernel,
        out_shape=outs,
        in_specs=[VMEM] * n_in,
        out_specs=[VMEM] * len(outs),
        scratch_shapes=[pltpu.VMEM(s.shape, s.dtype) for s in scratch],
        compiler_params=pltpu.CompilerParams(vmem_limit_bytes=min(held + 16 * MIB, 58 * MIB)),
        cost_estimate=pl.CostEstimate(flops=flops, bytes_accessed=moved, transcendentals=0),
        name=name,
    )


def exchange(x, axis, q):
    size = lax.axis_size(axis)
    return lax.ppermute(x, axis, [(i, i ^ q) for i in range(size)])


def shards(a_tiles, b_tiles, a_slots, b_slots):
    a_local = a_tiles.reshape(-1, FLAT)
    b_local = b_tiles.reshape(-1, FLAT)
    a_index = a_slots.reshape(1, -1)
    b_index = b_slots.reshape(1, -1)
    rows, cols, layers = lax.axis_size("row"), lax.axis_size("col"), lax.axis_size("layer")
    left_each, right_each = a_local.shape[0], b_local.shape[0]
    left_tiles = cols * left_each
    tiles = a_index.shape[1] // TASKS
    owned = tiles // layers
    pairs = right_each * left_tiles
    assert rows == 4 and layers == len(OWNER_ORDER)

    b_far = exchange(b_local, "row", 2)
    if cols == 2:
        a_parts = [a_local, exchange(a_local, "col", 1)]
    else:
        a_parts = [lax.all_gather(a_local, "col", axis=0, tiled=True)]
    (b_here,) = call(stage_kernel, [shape(b_local.shape, BF16)], [], 1, "stage", STAGE_FLOPS, MIB)(b_local)
    b_near = exchange(b_local, "row", 1)
    b_last = exchange(b_here, "row", 3)
    (sel,) = call(
        functools.partial(counts_kernel, cols == 2, left_tiles, left_each, right_each),
        [shape((tiles, rows * pairs), BF16)],
        [],
        2,
        "counts",
        2 * tiles * tiles * TASKS * TASKS,
        MIB,
    )(a_index, b_index)

    groups = (2,) if pairs * FLAT * 2 < 4 * MIB else (1, 1)
    raw = shape((right_each * LINES, LANES), F32)
    one = shape((LINES, pairs, LANES), BF16)
    shard_flops = 2 * pairs * LINES * LANES * LANES + 2 * pairs * tiles * FLAT
    acc, a_lines = call(
        functools.partial(own_kernel, groups, len(a_parts)),
        [shape((tiles, FLAT), F32), shape((left_tiles * LINES, LANES), BF16)],
        [raw, shape((LINES, max(groups) * pairs, LANES), BF16)],
        3 + len(a_parts),
        "own_and_near",
        2 * shard_flops,
        8 * MIB,
    )(sel, *a_parts, b_here, b_near)
    (acc,) = call(
        functools.partial(more_kernel, 2 * pairs),
        [shape((tiles, FLAT), F32)],
        [raw, one],
        4,
        "far_shard",
        shard_flops,
        4 * MIB,
    )(sel, a_lines, acc, b_far)
    half, width = LINES // 2, FLAT // 2
    results = []
    for first_line in (0, half):
        own, far, sent = call(
            functools.partial(last_kernel, 3 * pairs, first_line),
            [shape((owned, width), F32)] * 2 + [shape((2 * owned, width), BF16)],
            [raw, shape((half, pairs, LANES), BF16)],
            4,
            "last_shard",
            shard_flops // 2,
            2 * MIB,
        )(sel, a_lines, acc, b_last)
        arrived = exchange(sent, "layer", 1)
        (joined,) = call(
            join_kernel, [shape((owned, width), BF16)], [], 2, "join_cores", owned * width, MIB
        )(far, arrived)
        results += [own, arrived, exchange(joined, "layer", 2)]
    (out,) = call(
        add_kernel, [shape((owned, FLAT), BF16)], [], len(results), "add_layers", 2 * owned * FLAT, MIB
    )(*results)
    return out.reshape(1, 1, owned, FLAT)


def solution(mesh):
    in_specs = (
        P("row", "layer", "col", None, None),
        P("layer", "row", "col", None, None),
        P("row", "col", "layer", None),
        P("row", "col", "layer", None),
    )
    out_specs = P("row", "col", "layer", None)
    return jax.shard_map(shards, mesh=mesh, in_specs=in_specs, out_specs=out_specs, check_vma=False)
```

```python
import functools

import jax
import jax.numpy as jnp
from jax import lax
from jax.experimental import pallas as pl
from jax.experimental.pallas import tpu as pltpu
from jax.sharding import PartitionSpec as P

TILE = 64
TASKS = 8
FLAT = TILE * TILE
LANES = 128
LINES = FLAT // LANES
ROWS_AT_ONCE = 512
TILES_AT_ONCE = 4
LINES_AT_ONCE = 4
MIB = 1 << 20
OWN_FLOPS = 500 * 10**6
STAGE_FLOPS = 2 * 10**9
F32, BF16 = jnp.float32, jnp.bfloat16
OWNER_ORDER = (0, 2, 3, 1)


def iota(shape, axis):
    return lax.broadcasted_iota(jnp.int32, shape, axis)


def ones_where(hit):
    return jnp.where(hit, 1.0, 0.0).astype(BF16)


def split_inner_order():
    src, dst = iota((LANES, LANES), 0), iota((LANES, LANES), 1)
    half, rest = dst // TILE, dst % TILE
    wanted = half * TILE + 2 * (rest % (TILE // 2)) + rest // (TILE // 2)
    return ones_where(src == wanted)


def twice_on_diagonal(lines):
    low = ones_where(iota(lines.shape, 1) < TILE)
    high = ones_where(iota(lines.shape, 1) >= TILE)
    turned = pltpu.roll(lines, TILE, 1).astype(BF16)
    lines = lines.astype(BF16)
    return jnp.concatenate([lines * low, turned * low, turned * high, lines * high], axis=0)


def loop(count, few, body):
    if count <= few:
        for i in range(count):
            body(i)
    else:
        pl.loop(0, count)(body)


def stage_kernel(*refs):
    for ref, out in zip(refs[:len(refs) // 2], refs[len(refs) // 2:]):
        out[...] = ref[...]


def counts_kernel(swap, left_tiles, left_each, right_each, a_slots, b_slots, sel):
    row, col, layer = lax.axis_index("row"), lax.axis_index("col"), lax.axis_index("layer")
    tiles, pairs = sel.shape
    tasks = tiles * TASKS
    owned = tiles // len(OWNER_ORDER)
    place = iota((tiles, tasks), 0)
    group = place // owned
    owner = jnp.zeros_like(group)
    for g, q in enumerate(OWNER_ORDER):
        owner = jnp.where(group == g, q, owner)
    tile = (owner ^ layer) * owned + place % owned
    mine = jnp.where(iota((tiles, tasks), 1) // TASKS == tile, 1.0, 0.0).astype(BF16)
    entry = iota((2 * TASKS, tasks), 0)
    at = iota((2 * TASKS, tasks), 1) % TASKS
    a_index, b_index = a_slots[...], b_slots[...]
    a_place = a_index ^ (col * left_each) if swap else a_index
    a_place = jnp.where(a_index < left_tiles, a_place, left_tiles)
    b_place = ((b_index // right_each) ^ row) * right_each + b_index % right_each
    spread = jnp.where(at == entry, a_place, 0) + jnp.where(at + TASKS == entry, b_place, 0)
    lists = lax.dot_general(
        mine, spread.astype(F32).astype(BF16), (((1,), (1,)), ((), ())), preferred_element_type=F32
    ).astype(jnp.int32)
    width = min(pairs, 1024)

    def some(part):
        here = iota((tiles, width), 1) + part * width
        total = jnp.zeros((tiles, width), F32)
        for e in range(TASKS):
            a_at, b_at = lists[:, e:e + 1], lists[:, TASKS + e:TASKS + e + 1]
            pair = jnp.where(a_at < left_tiles, b_at * left_tiles + a_at, -1)
            total = total + jnp.where(here == pair, 1.0, 0.0)
        sel[:, pl.ds(pl.multiple_of(part * width, width), width)] = total.astype(BF16)

    loop(pairs // width, 1, some)


def left_lines(a_refs, a_lines):
    order = split_inner_order()
    left_tiles = sum(r.shape[0] for r in a_refs)
    lines_at_once = min(LINES, max(1, ROWS_AT_ONCE // left_tiles))
    for i in range(0, LINES, lines_at_once):
        block = jnp.concatenate(
            [
                r[:, j * LANES:(j + 1) * LANES].astype(F32)
                for j in range(i, i + lines_at_once)
                for r in a_refs
            ],
            axis=0,
        ).astype(BF16)
        got = jnp.dot(block, order, preferred_element_type=F32)
        a_lines[i * left_tiles:(i + lines_at_once) * left_tiles, :] = got.astype(BF16)


def all_products(a_lines, b_ref, raw, prod, first, first_line=0):
    right_tiles = b_ref.shape[0]
    left_tiles = a_lines.shape[0] // LINES
    for i in range(LINES):
        raw[i * right_tiles:(i + 1) * right_tiles, :] = b_ref[:, i * LANES:(i + 1) * LANES].astype(F32)
    lines = prod.shape[0]
    lines_at_once = min(lines, max(1, ROWS_AT_ONCE // left_tiles))
    rows = lines_at_once * left_tiles

    def some_tiles(p):
        right = jnp.concatenate(
            [
                twice_on_diagonal(raw[pl.ds(p * TILES_AT_ONCE + h, LINES, stride=right_tiles), :])
                for h in range(TILES_AT_ONCE)
            ],
            axis=1,
        )

        def some(part):
            at = first_line * left_tiles + part * rows
            at = at if isinstance(at, int) else pl.multiple_of(at, rows)
            got = jnp.dot(a_lines[pl.ds(at, rows), :], right, preferred_element_type=F32).astype(BF16)
            for j in range(lines_at_once):
                for h in range(TILES_AT_ONCE):
                    to = first + (p * TILES_AT_ONCE + h) * left_tiles
                    to = to if isinstance(to, int) else pl.multiple_of(to, left_tiles)
                    prod[part * lines_at_once + j, pl.ds(to, left_tiles), :] = got[
                        j * left_tiles:(j + 1) * left_tiles, h * LANES:(h + 1) * LANES
                    ]

        loop(lines // lines_at_once, 1, some)

    loop(right_tiles // TILES_AT_ONCE, 8 if lines == lines_at_once else 1, some_tiles)


def chosen_sums(sel, first, count, prod, put):
    for j in range(0, prod.shape[0], LINES_AT_ONCE):
        right = jnp.concatenate([prod[j + i, :count, :] for i in range(LINES_AT_ONCE)], axis=1)
        put(
            slice(j * LANES, (j + LINES_AT_ONCE) * LANES),
            jnp.dot(sel[:, first:first + count], right, preferred_element_type=F32),
        )


def own_kernel(groups, n_left, sel, *refs):
    shards = sum(groups)
    a_refs, b_refs = refs[:n_left], refs[n_left:n_left + shards]
    acc, a_lines, raw, prod = refs[n_left + shards:]
    left_lines(a_refs, a_lines)
    add_shards(0, groups, sel, a_lines, b_refs, None, acc, raw, prod)


def more_kernel(start, sel, a_lines, acc, b_ref, out, raw, prod):
    add_shards(start, (1,), sel, a_lines, (b_ref,), acc, out, raw, prod)


def add_shards(start, groups, sel, a_lines, b_refs, acc, out, raw, prod):
    each = a_lines.shape[0] // LINES
    taken = 0
    for count in groups:
        done = 0
        before = out if taken else acc
        for b_ref in b_refs[taken:taken + count]:
            all_products(a_lines, b_ref, raw, prod, done)
            done += b_ref.shape[0] * each

        def put(columns, value):
            out[:, columns] = value if before is None else value + before[:, columns]

        chosen_sums(sel, start, done, prod, put)
        taken += count
        start += done


def last_kernel(start, first_line, sel, a_lines, acc, b_ref, own, far, sent, raw, prod):
    pairs = b_ref.shape[0] * a_lines.shape[0] // LINES
    owned = own.shape[0]
    all_products(a_lines, b_ref, raw, prod, 0, first_line)

    def put(columns, value):
        value = value + acc[:, first_line * LANES + columns.start:first_line * LANES + columns.stop]
        own[:, columns] = value[:owned]
        far[:, columns] = value[owned:2 * owned]
        sent[:, columns] = value[2 * owned:].astype(sent.dtype)

    chosen_sums(sel, start, pairs, prod, put)


def join_kernel(far, arrived, out):
    out[...] = (far[...] + arrived[:out.shape[0], :].astype(F32)).astype(out.dtype)


def add_kernel(*refs):
    out = refs[-1]
    count, done = out.shape[0], 0
    for own, arrived, joined in zip(refs[0:-1:3], refs[1:-1:3], refs[2:-1:3]):
        total = own[...] + arrived[count:, :].astype(F32) + joined[...].astype(F32)
        out[:, done:done + total.shape[1]] = total.astype(out.dtype)
        done += total.shape[1]


VMEM = pl.BlockSpec(memory_space=pltpu.VMEM)


def shape(dims, kind):
    return jax.ShapeDtypeStruct(dims, kind)


def call(kernel, outs, scratch, n_in, name, flops, moved):
    held = sum(s.dtype.itemsize * functools.reduce(lambda x, y: x * y, s.shape) for s in outs + scratch)
    return pl.pallas_call(
        kernel,
        out_shape=outs,
        in_specs=[VMEM] * n_in,
        out_specs=[VMEM] * len(outs),
        scratch_shapes=[pltpu.VMEM(s.shape, s.dtype) for s in scratch],
        compiler_params=pltpu.CompilerParams(vmem_limit_bytes=min(held + 16 * MIB, 58 * MIB)),
        cost_estimate=pl.CostEstimate(flops=flops, bytes_accessed=moved, transcendentals=0),
        name=name,
    )


def exchange(x, axis, q):
    size = lax.axis_size(axis)
    return lax.ppermute(x, axis, [(i, i ^ q) for i in range(size)])


def shards(a_tiles, b_tiles, a_slots, b_slots):
    a_local = a_tiles.reshape(-1, FLAT)
    b_local = b_tiles.reshape(-1, FLAT)
    a_index = a_slots.reshape(1, -1)
    b_index = b_slots.reshape(1, -1)
    rows, cols, layers = lax.axis_size("row"), lax.axis_size("col"), lax.axis_size("layer")
    left_each, right_each = a_local.shape[0], b_local.shape[0]
    left_tiles = cols * left_each
    tiles = a_index.shape[1] // TASKS
    owned = tiles // layers
    pairs = right_each * left_tiles
    assert rows == 4 and layers == len(OWNER_ORDER)

    b_far = exchange(b_local, "row", 2)
    if cols == 2:
        a_parts = [a_local, exchange(a_local, "col", 1)]
    else:
        a_parts = [lax.all_gather(a_local, "col", axis=0, tiled=True)]
    (b_here,) = call(stage_kernel, [shape(b_local.shape, BF16)], [], 1, "stage", STAGE_FLOPS, MIB)(b_local)
    b_near = exchange(b_local, "row", 1)
    b_last = exchange(b_local, "row", 3)
    (sel,) = call(
        functools.partial(counts_kernel, cols == 2, left_tiles, left_each, right_each),
        [shape((tiles, rows * pairs), BF16)],
        [],
        2,
        "counts",
        2 * tiles * tiles * TASKS * TASKS,
        MIB,
    )(a_index, b_index)

    raw = shape((right_each * LINES, LANES), F32)
    one = shape((LINES, pairs, LANES), BF16)
    shard_flops = 2 * pairs * LINES * LANES * LANES + 2 * pairs * tiles * FLAT
    acc, a_lines = call(
        functools.partial(own_kernel, (1,), len(a_parts)),
        [shape((tiles, FLAT), F32), shape((left_tiles * LINES, LANES), BF16)],
        [raw, one],
        2 + len(a_parts),
        "own_shard",
        OWN_FLOPS,
        4 * MIB,
    )(sel, *a_parts, b_here)
    for name, m, b_shard in (("far_shard", 2, b_far), ("near_shard", 1, b_near)):
        (acc,) = call(
            functools.partial(more_kernel, m * pairs),
            [shape((tiles, FLAT), F32)],
            [raw, one],
            4,
            name,
            shard_flops,
            4 * MIB,
        )(sel, a_lines, acc, b_shard)
    results = []
    for first_line, lines in ((0, LINES // 4), (LINES // 4, 3 * LINES // 4)):
        width = lines * LANES
        own, far, sent = call(
            functools.partial(last_kernel, 3 * pairs, first_line),
            [shape((owned, width), F32)] * 2 + [shape((2 * owned, width), BF16)],
            [raw, shape((lines, pairs, LANES), BF16)],
            4,
            "last_shard",
            shard_flops * lines // LINES,
            2 * MIB,
        )(sel, a_lines, acc, b_last)
        arrived = exchange(sent, "layer", 1)
        (joined,) = call(
            join_kernel, [shape((owned, width), BF16)], [], 2, "join_cores", owned * width, MIB
        )(far, arrived)
        results += [own, arrived, exchange(joined, "layer", 2)]
    (out,) = call(
        add_kernel, [shape((owned, FLAT), BF16)], [], len(results), "add_layers", 2 * owned * FLAT, MIB
    )(*results)
    return out.reshape(1, 1, owned, FLAT)


def solution(mesh):
    in_specs = (
        P("row", "layer", "col", None, None),
        P("layer", "row", "col", None, None),
        P("row", "col", "layer", None),
        P("row", "col", "layer", None),
    )
    out_specs = P("row", "col", "layer", None)
    return jax.shard_map(shards, mesh=mesh, in_specs=in_specs, out_specs=out_specs, check_vma=False)
```

```python
import functools

import jax
import jax.numpy as jnp
from jax import lax
from jax.experimental import pallas as pl
from jax.experimental.pallas import tpu as pltpu
from jax.sharding import PartitionSpec as P

TILE = 64
TASKS = 8
FLAT = TILE * TILE
LANES = 128
LINES = FLAT // LANES
ROWS_AT_ONCE = 512
FIRST_LINES = LINES // 2
TILES_AT_ONCE = 4
LINES_AT_ONCE = 4
MIB = 1 << 20
OWN_FLOPS = 500 * 10**6
STAGE_FLOPS = 2 * 10**9
F32, BF16 = jnp.float32, jnp.bfloat16
OWNER_ORDER = (0, 2, 3, 1)


def iota(shape, axis):
    return lax.broadcasted_iota(jnp.int32, shape, axis)


def ones_where(hit):
    return jnp.where(hit, 1.0, 0.0).astype(BF16)


def split_inner_order():
    src, dst = iota((LANES, LANES), 0), iota((LANES, LANES), 1)
    half, rest = dst // TILE, dst % TILE
    wanted = half * TILE + 2 * (rest % (TILE // 2)) + rest // (TILE // 2)
    return ones_where(src == wanted)


def twice_on_diagonal(lines):
    low = ones_where(iota(lines.shape, 1) < TILE)
    high = ones_where(iota(lines.shape, 1) >= TILE)
    turned = pltpu.roll(lines, TILE, 1).astype(BF16)
    lines = lines.astype(BF16)
    return jnp.concatenate([lines * low, turned * low, turned * high, lines * high], axis=0)


def loop(count, few, body):
    if count <= few:
        for i in range(count):
            body(i)
    else:
        pl.loop(0, count)(body)


def stage_kernel(*refs):
    for ref, out in zip(refs[:len(refs) // 2], refs[len(refs) // 2:]):
        out[...] = ref[...]


def counts_kernel(swap, left_tiles, left_each, right_each, a_slots, b_slots, sel):
    row, col, layer = lax.axis_index("row"), lax.axis_index("col"), lax.axis_index("layer")
    tiles, pairs = sel.shape
    tasks = tiles * TASKS
    owned = tiles // len(OWNER_ORDER)
    place = iota((tiles, tasks), 0)
    group = place // owned
    owner = jnp.zeros_like(group)
    for g, q in enumerate(OWNER_ORDER):
        owner = jnp.where(group == g, q, owner)
    tile = (owner ^ layer) * owned + place % owned
    mine = jnp.where(iota((tiles, tasks), 1) // TASKS == tile, 1.0, 0.0).astype(BF16)
    entry = iota((2 * TASKS, tasks), 0)
    at = iota((2 * TASKS, tasks), 1) % TASKS
    a_index, b_index = a_slots[...], b_slots[...]
    a_place = a_index ^ (col * left_each) if swap else a_index
    a_place = jnp.where(a_index < left_tiles, a_place, left_tiles)
    b_place = ((b_index // right_each) ^ row) * right_each + b_index % right_each
    spread = jnp.where(at == entry, a_place, 0) + jnp.where(at + TASKS == entry, b_place, 0)
    lists = lax.dot_general(
        mine, spread.astype(F32).astype(BF16), (((1,), (1,)), ((), ())), preferred_element_type=F32
    ).astype(jnp.int32)
    width = min(pairs, 1024)

    def some(part):
        here = iota((tiles, width), 1) + part * width
        total = jnp.zeros((tiles, width), F32)
        for e in range(TASKS):
            a_at, b_at = lists[:, e:e + 1], lists[:, TASKS + e:TASKS + e + 1]
            pair = jnp.where(a_at < left_tiles, b_at * left_tiles + a_at, -1)
            total = total + jnp.where(here == pair, 1.0, 0.0)
        sel[:, pl.ds(pl.multiple_of(part * width, width), width)] = total.astype(BF16)

    loop(pairs // width, 1, some)


def left_lines(a_refs, a_lines):
    order = split_inner_order()
    left_tiles = sum(r.shape[0] for r in a_refs)
    lines_at_once = min(LINES, max(1, ROWS_AT_ONCE // left_tiles))
    for i in range(0, LINES, lines_at_once):
        block = jnp.concatenate(
            [
                r[:, j * LANES:(j + 1) * LANES].astype(F32)
                for j in range(i, i + lines_at_once)
                for r in a_refs
            ],
            axis=0,
        ).astype(BF16)
        got = jnp.dot(block, order, preferred_element_type=F32)
        a_lines[i * left_tiles:(i + lines_at_once) * left_tiles, :] = got.astype(BF16)


def all_products(a_lines, b_ref, raw, prod, first, first_line=0, rights=None):
    right_tiles = b_ref.shape[0]
    left_tiles = a_lines.shape[0] // LINES
    for i in range(LINES if raw is not None else 0):
        raw[i * right_tiles:(i + 1) * right_tiles, :] = b_ref[:, i * LANES:(i + 1) * LANES].astype(F32)
    lines = prod.shape[0]
    lines_at_once = min(lines, max(1, ROWS_AT_ONCE // left_tiles))
    rows = lines_at_once * left_tiles

    def some_tiles(p):
        columns = p * TILES_AT_ONCE * LANES
        columns = columns if isinstance(columns, int) else pl.multiple_of(columns, TILES_AT_ONCE * LANES)
        columns = pl.ds(columns, TILES_AT_ONCE * LANES)
        if raw is None:
            right = rights[:, columns]
        else:
            right = jnp.concatenate(
                [
                    twice_on_diagonal(raw[pl.ds(p * TILES_AT_ONCE + h, LINES, stride=right_tiles), :])
                    for h in range(TILES_AT_ONCE)
                ],
                axis=1,
            )
            if rights is not None:
                rights[:, columns] = right

        def some(part):
            at = first_line * left_tiles + part * rows
            at = at if isinstance(at, int) else pl.multiple_of(at, rows)
            got = jnp.dot(a_lines[pl.ds(at, rows), :], right, preferred_element_type=F32).astype(BF16)
            for j in range(lines_at_once):
                for h in range(TILES_AT_ONCE):
                    to = first + (p * TILES_AT_ONCE + h) * left_tiles
                    to = to if isinstance(to, int) else pl.multiple_of(to, left_tiles)
                    prod[part * lines_at_once + j, pl.ds(to, left_tiles), :] = got[
                        j * left_tiles:(j + 1) * left_tiles, h * LANES:(h + 1) * LANES
                    ]

        loop(lines // lines_at_once, 1, some)

    loop(right_tiles // TILES_AT_ONCE, 8 if lines == lines_at_once else 1, some_tiles)


def chosen_sums(sel, first, count, prod, put):
    for j in range(0, prod.shape[0], LINES_AT_ONCE):
        right = jnp.concatenate([prod[j + i, :count, :] for i in range(LINES_AT_ONCE)], axis=1)
        put(
            slice(j * LANES, (j + LINES_AT_ONCE) * LANES),
            jnp.dot(sel[:, first:first + count], right, preferred_element_type=F32),
        )


def own_kernel(groups, n_left, sel, *refs):
    shards = sum(groups)
    a_refs, b_refs = refs[:n_left], refs[n_left:n_left + shards]
    acc, a_lines, raw, prod = refs[n_left + shards:]
    left_lines(a_refs, a_lines)
    add_shards(0, groups, sel, a_lines, b_refs, None, acc, raw, prod)


def more_kernel(start, sel, a_lines, acc, b_ref, out, raw, prod):
    add_shards(start, (1,), sel, a_lines, (b_ref,), acc, out, raw, prod)


def add_shards(start, groups, sel, a_lines, b_refs, acc, out, raw, prod):
    each = a_lines.shape[0] // LINES
    taken = 0
    for count in groups:
        done = 0
        before = out if taken else acc
        for b_ref in b_refs[taken:taken + count]:
            all_products(a_lines, b_ref, raw, prod, done)
            done += b_ref.shape[0] * each

        def put(columns, value):
            out[:, columns] = value if before is None else value + before[:, columns]

        chosen_sums(sel, start, done, prod, put)
        taken += count
        start += done


def last_kernel(start, first_line, sel, a_lines, acc, b_ref, *refs):
    if first_line:
        (rights, own, far, sent, prod), raw = refs, None
    else:
        own, far, sent, rights, raw, prod = refs
    pairs = b_ref.shape[0] * a_lines.shape[0] // LINES
    owned = own.shape[0]
    all_products(a_lines, b_ref, raw, prod, 0, first_line, rights)

    def put(columns, value):
        value = value + acc[:, first_line * LANES + columns.start:first_line * LANES + columns.stop]
        own[:, columns] = value[:owned]
        far[:, columns] = value[owned:2 * owned]
        sent[:, columns] = value[2 * owned:].astype(sent.dtype)

    chosen_sums(sel, start, pairs, prod, put)


def join_kernel(far, arrived, out):
    out[...] = (far[...] + arrived[:out.shape[0], :].astype(F32)).astype(out.dtype)


def add_kernel(*refs):
    out = refs[-1]
    count, done = out.shape[0], 0
    for own, arrived, joined in zip(refs[0:-1:3], refs[1:-1:3], refs[2:-1:3]):
        total = own[...] + arrived[count:, :].astype(F32) + joined[...].astype(F32)
        out[:, done:done + total.shape[1]] = total.astype(out.dtype)
        done += total.shape[1]


VMEM = pl.BlockSpec(memory_space=pltpu.VMEM)


def shape(dims, kind):
    return jax.ShapeDtypeStruct(dims, kind)


def call(kernel, outs, scratch, n_in, name, flops, moved):
    held = sum(s.dtype.itemsize * functools.reduce(lambda x, y: x * y, s.shape) for s in outs + scratch)
    return pl.pallas_call(
        kernel,
        out_shape=outs,
        in_specs=[VMEM] * n_in,
        out_specs=[VMEM] * len(outs),
        scratch_shapes=[pltpu.VMEM(s.shape, s.dtype) for s in scratch],
        compiler_params=pltpu.CompilerParams(vmem_limit_bytes=min(held + 16 * MIB, 58 * MIB)),
        cost_estimate=pl.CostEstimate(flops=flops, bytes_accessed=moved, transcendentals=0),
        name=name,
    )


def exchange(x, axis, q):
    size = lax.axis_size(axis)
    return lax.ppermute(x, axis, [(i, i ^ q) for i in range(size)])


def shards(a_tiles, b_tiles, a_slots, b_slots):
    a_local = a_tiles.reshape(-1, FLAT)
    b_local = b_tiles.reshape(-1, FLAT)
    a_index = a_slots.reshape(1, -1)
    b_index = b_slots.reshape(1, -1)
    rows, cols, layers = lax.axis_size("row"), lax.axis_size("col"), lax.axis_size("layer")
    left_each, right_each = a_local.shape[0], b_local.shape[0]
    left_tiles = cols * left_each
    tiles = a_index.shape[1] // TASKS
    owned = tiles // layers
    pairs = right_each * left_tiles
    assert rows == 4 and layers == len(OWNER_ORDER)

    b_far = exchange(b_local, "row", 2)
    if cols == 2:
        a_parts = [a_local, exchange(a_local, "col", 1)]
    else:
        a_parts = [lax.all_gather(a_local, "col", axis=0, tiled=True)]
    (b_here,) = call(stage_kernel, [shape(b_local.shape, BF16)], [], 1, "stage", STAGE_FLOPS, MIB)(b_local)
    b_near = exchange(b_local, "row", 1)
    b_last = exchange(b_local, "row", 3)
    (sel,) = call(
        functools.partial(counts_kernel, cols == 2, left_tiles, left_each, right_each),
        [shape((tiles, rows * pairs), BF16)],
        [],
        2,
        "counts",
        2 * tiles * tiles * TASKS * TASKS,
        MIB,
    )(a_index, b_index)

    raw = shape((right_each * LINES, LANES), F32)
    one = shape((LINES, pairs, LANES), BF16)
    shard_flops = 2 * pairs * LINES * LANES * LANES + 2 * pairs * tiles * FLAT
    acc, a_lines = call(
        functools.partial(own_kernel, (1,), len(a_parts)),
        [shape((tiles, FLAT), F32), shape((left_tiles * LINES, LANES), BF16)],
        [raw, one],
        2 + len(a_parts),
        "own_shard",
        OWN_FLOPS,
        4 * MIB,
    )(sel, *a_parts, b_here)
    for name, m, b_shard in (("far_shard", 2, b_far), ("near_shard", 1, b_near)):
        (acc,) = call(
            functools.partial(more_kernel, m * pairs),
            [shape((tiles, FLAT), F32)],
            [raw, one],
            4,
            name,
            shard_flops,
            4 * MIB,
        )(sel, a_lines, acc, b_shard)
    results, kept = [], []
    for first_line, lines in ((0, FIRST_LINES), (FIRST_LINES, LINES - FIRST_LINES)):
        width = lines * LANES
        outs = [shape((owned, width), F32)] * 2 + [shape((2 * owned, width), BF16)]
        if not kept:
            outs += [shape((LANES, right_each * LANES), BF16)]
        own, far, sent, *made = call(
            functools.partial(last_kernel, 3 * pairs, first_line),
            outs,
            ([] if kept else [raw]) + [shape((lines, pairs, LANES), BF16)],
            4 + len(kept),
            "last_shard",
            shard_flops * lines // LINES,
            2 * MIB,
        )(sel, a_lines, acc, b_last, *kept)
        kept = kept or made
        arrived = exchange(sent, "layer", 1)
        (joined,) = call(
            join_kernel, [shape((owned, width), BF16)], [], 2, "join_cores", owned * width, MIB
        )(far, arrived)
        results += [own, arrived, exchange(joined, "layer", 2)]
    (out,) = call(
        add_kernel, [shape((owned, FLAT), BF16)], [], len(results), "add_layers", 2 * owned * FLAT, MIB
    )(*results)
    return out.reshape(1, 1, owned, FLAT)


def solution(mesh):
    in_specs = (
        P("row", "layer", "col", None, None),
        P("layer", "row", "col", None, None),
        P("row", "col", "layer", None),
        P("row", "col", "layer", None),
    )
    out_specs = P("row", "col", "layer", None)
    return jax.shard_map(shards, mesh=mesh, in_specs=in_specs, out_specs=out_specs, check_vma=False)
```

```python
import functools

import jax
import jax.numpy as jnp
from jax import lax
from jax.experimental import pallas as pl
from jax.experimental.pallas import tpu as pltpu
from jax.sharding import PartitionSpec as P

TILE = 64
TASKS = 8
FLAT = TILE * TILE
LANES = 128
LINES = FLAT // LANES
ROWS_AT_ONCE = 512
FIRST_LINES = LINES // 2
TILES_AT_ONCE = 4
LINES_AT_ONCE = 4
MIB = 1 << 20
OWN_FLOPS = 500 * 10**6
STAGE_FLOPS = 2 * 10**9
F32, BF16 = jnp.float32, jnp.bfloat16
OWNER_ORDER = (0, 2, 3, 1)


def iota(shape, axis):
    return lax.broadcasted_iota(jnp.int32, shape, axis)


def ones_where(hit):
    return jnp.where(hit, 1.0, 0.0).astype(BF16)


def split_inner_order():
    src, dst = iota((LANES, LANES), 0), iota((LANES, LANES), 1)
    half, rest = dst // TILE, dst % TILE
    wanted = half * TILE + 2 * (rest % (TILE // 2)) + rest // (TILE // 2)
    return ones_where(src == wanted)


def twice_on_diagonal(lines):
    low = ones_where(iota(lines.shape, 1) < TILE)
    high = ones_where(iota(lines.shape, 1) >= TILE)
    turned = pltpu.roll(lines, TILE, 1).astype(BF16)
    lines = lines.astype(BF16)
    return jnp.concatenate([lines * low, turned * low, turned * high, lines * high], axis=0)


def loop(count, few, body):
    if count <= few:
        for i in range(count):
            body(i)
    else:
        pl.loop(0, count)(body)


def stage_kernel(*refs):
    for ref, out in zip(refs[:len(refs) // 2], refs[len(refs) // 2:]):
        out[...] = ref[...]


def counts_kernel(swap, left_tiles, left_each, right_each, a_slots, b_slots, sel):
    row, col, layer = lax.axis_index("row"), lax.axis_index("col"), lax.axis_index("layer")
    tiles, pairs = sel.shape
    tasks = tiles * TASKS
    owned = tiles // len(OWNER_ORDER)
    place = iota((tiles, tasks), 0)
    group = place // owned
    owner = jnp.zeros_like(group)
    for g, q in enumerate(OWNER_ORDER):
        owner = jnp.where(group == g, q, owner)
    tile = (owner ^ layer) * owned + place % owned
    mine = jnp.where(iota((tiles, tasks), 1) // TASKS == tile, 1.0, 0.0).astype(BF16)
    entry = iota((2 * TASKS, tasks), 0)
    at = iota((2 * TASKS, tasks), 1) % TASKS
    a_index, b_index = a_slots[...], b_slots[...]
    a_place = a_index ^ (col * left_each) if swap else a_index
    a_place = jnp.where(a_index < left_tiles, a_place, left_tiles)
    b_place = ((b_index // right_each) ^ row) * right_each + b_index % right_each
    spread = jnp.where(at == entry, a_place, 0) + jnp.where(at + TASKS == entry, b_place, 0)
    lists = lax.dot_general(
        mine, spread.astype(F32).astype(BF16), (((1,), (1,)), ((), ())), preferred_element_type=F32
    ).astype(jnp.int32)
    width = min(pairs, 1024)

    def some(part):
        here = iota((tiles, width), 1) + part * width
        total = jnp.zeros((tiles, width), F32)
        for e in range(TASKS):
            a_at, b_at = lists[:, e:e + 1], lists[:, TASKS + e:TASKS + e + 1]
            pair = jnp.where(a_at < left_tiles, b_at * left_tiles + a_at, -1)
            total = total + jnp.where(here == pair, 1.0, 0.0)
        sel[:, pl.ds(pl.multiple_of(part * width, width), width)] = total.astype(BF16)

    loop(pairs // width, 1, some)


def left_lines(a_refs, a_lines):
    order = split_inner_order()
    left_tiles = sum(r.shape[0] for r in a_refs)
    lines_at_once = min(LINES, max(1, ROWS_AT_ONCE // left_tiles))
    for i in range(0, LINES, lines_at_once):
        block = jnp.concatenate(
            [
                r[:, j * LANES:(j + 1) * LANES].astype(F32)
                for j in range(i, i + lines_at_once)
                for r in a_refs
            ],
            axis=0,
        ).astype(BF16)
        got = jnp.dot(block, order, preferred_element_type=F32)
        a_lines[i * left_tiles:(i + lines_at_once) * left_tiles, :] = got.astype(BF16)


def all_products(a_lines, b_ref, raw, prod, first, first_line=0, rights=None):
    right_tiles = b_ref.shape[0]
    left_tiles = a_lines.shape[0] // LINES
    for i in range(LINES if raw is not None else 0):
        raw[i * right_tiles:(i + 1) * right_tiles, :] = b_ref[:, i * LANES:(i + 1) * LANES].astype(F32)
    lines = prod.shape[0]
    lines_at_once = min(lines, max(1, ROWS_AT_ONCE // left_tiles))
    rows = lines_at_once * left_tiles

    def some_tiles(p):
        columns = p * TILES_AT_ONCE * LANES
        columns = columns if isinstance(columns, int) else pl.multiple_of(columns, TILES_AT_ONCE * LANES)
        columns = pl.ds(columns, TILES_AT_ONCE * LANES)
        if raw is None:
            right = rights[:, columns]
        else:
            right = jnp.concatenate(
                [
                    twice_on_diagonal(raw[pl.ds(p * TILES_AT_ONCE + h, LINES, stride=right_tiles), :])
                    for h in range(TILES_AT_ONCE)
                ],
                axis=1,
            )
            if rights is not None:
                rights[:, columns] = right

        def some(part):
            at = first_line * left_tiles + part * rows
            at = at if isinstance(at, int) else pl.multiple_of(at, rows)
            got = jnp.dot(a_lines[pl.ds(at, rows), :], right, preferred_element_type=F32).astype(BF16)
            for j in range(lines_at_once):
                for h in range(TILES_AT_ONCE):
                    to = first + (p * TILES_AT_ONCE + h) * left_tiles
                    to = to if isinstance(to, int) else pl.multiple_of(to, left_tiles)
                    prod[part * lines_at_once + j, pl.ds(to, left_tiles), :] = got[
                        j * left_tiles:(j + 1) * left_tiles, h * LANES:(h + 1) * LANES
                    ]

        loop(lines // lines_at_once, 1, some)

    loop(right_tiles // TILES_AT_ONCE, 8 if lines == lines_at_once else 1, some_tiles)


def chosen_sums(sel, first, count, prod, put):
    for j in range(0, prod.shape[0], LINES_AT_ONCE):
        right = jnp.concatenate([prod[j + i, :count, :] for i in range(LINES_AT_ONCE)], axis=1)
        put(
            slice(j * LANES, (j + LINES_AT_ONCE) * LANES),
            jnp.dot(sel[:, first:first + count], right, preferred_element_type=F32),
        )


def own_kernel(groups, n_left, sel, *refs):
    shards = sum(groups)
    a_refs, b_refs = refs[:n_left], refs[n_left:n_left + shards]
    acc, a_lines, raw, prod = refs[n_left + shards:]
    left_lines(a_refs, a_lines)
    add_shards(0, groups, sel, a_lines, b_refs, None, acc, raw, prod)


def more_kernel(start, groups, sel, a_lines, acc, *refs):
    b_refs, (out, raw, prod) = refs[-4::-1], refs[-3:]
    add_shards(start, groups, sel, a_lines, b_refs, acc, out, raw, prod)


def add_shards(start, groups, sel, a_lines, b_refs, acc, out, raw, prod):
    each = a_lines.shape[0] // LINES
    taken = 0
    for count in groups:
        done = 0
        before = out if taken else acc
        for b_ref in b_refs[taken:taken + count]:
            all_products(a_lines, b_ref, raw, prod, done)
            done += b_ref.shape[0] * each

        def put(columns, value):
            out[:, columns] = value if before is None else value + before[:, columns]

        chosen_sums(sel, start, done, prod, put)
        taken += count
        start += done


def last_kernel(start, first_line, sel, a_lines, acc, b_ref, *refs):
    if first_line:
        (rights, own, far, sent, prod), raw = refs, None
    else:
        own, far, sent, rights, raw, prod = refs
    pairs = b_ref.shape[0] * a_lines.shape[0] // LINES
    owned = own.shape[0]
    all_products(a_lines, b_ref, raw, prod, 0, first_line, rights)

    def put(columns, value):
        value = value + acc[:, first_line * LANES + columns.start:first_line * LANES + columns.stop]
        own[:, columns] = value[:owned]
        far[:, columns] = value[owned:2 * owned]
        sent[:, columns] = value[2 * owned:].astype(sent.dtype)

    chosen_sums(sel, start, pairs, prod, put)


def join_kernel(far, arrived, out):
    out[...] = (far[...] + arrived[:out.shape[0], :].astype(F32)).astype(out.dtype)


def add_kernel(first_column, own, arrived, joined, *refs):
    out, total, sem = refs[-3:]
    count, width = own.shape
    value = own[...] + arrived[count:, :].astype(F32) + joined[...].astype(F32)
    total[...] = value.astype(total.dtype)
    write = pltpu.make_async_copy(total, out.at[:, pl.ds(first_column, width)], sem)
    write.start()
    write.wait()


VMEM = pl.BlockSpec(memory_space=pltpu.VMEM)
HBM = pl.BlockSpec(memory_space=pltpu.HBM)


def shape(dims, kind):
    return jax.ShapeDtypeStruct(dims, kind)


def call(kernel, outs, scratch, n_in, name, flops, moved, in_place=None):
    held = sum(s.dtype.itemsize * functools.reduce(lambda x, y: x * y, s.shape) for s in outs + scratch)
    return pl.pallas_call(
        kernel,
        out_shape=outs,
        in_specs=[VMEM] * n_in + [HBM] * (in_place or 0),
        out_specs=[VMEM if in_place is None else HBM] * len(outs),
        scratch_shapes=[pltpu.VMEM(s.shape, s.dtype) for s in scratch]
        + ([] if in_place is None else [pltpu.SemaphoreType.DMA]),
        input_output_aliases={n_in: 0} if in_place else {},
        compiler_params=pltpu.CompilerParams(vmem_limit_bytes=min(held + 16 * MIB, 58 * MIB)),
        cost_estimate=pl.CostEstimate(flops=flops, bytes_accessed=moved, transcendentals=0),
        name=name,
    )


def exchange(x, axis, q):
    size = lax.axis_size(axis)
    return lax.ppermute(x, axis, [(i, i ^ q) for i in range(size)])


def shards(a_tiles, b_tiles, a_slots, b_slots):
    a_local = a_tiles.reshape(-1, FLAT)
    b_local = b_tiles.reshape(-1, FLAT)
    a_index = a_slots.reshape(1, -1)
    b_index = b_slots.reshape(1, -1)
    rows, cols, layers = lax.axis_size("row"), lax.axis_size("col"), lax.axis_size("layer")
    left_each, right_each = a_local.shape[0], b_local.shape[0]
    left_tiles = cols * left_each
    tiles = a_index.shape[1] // TASKS
    owned = tiles // layers
    pairs = right_each * left_tiles
    assert rows == 4 and layers == len(OWNER_ORDER)

    b_far = exchange(b_local, "row", 2)
    if cols == 2:
        a_parts = [a_local, exchange(a_local, "col", 1)]
    else:
        a_parts = [lax.all_gather(a_local, "col", axis=0, tiled=True)]
    (b_here,) = call(stage_kernel, [shape(b_local.shape, BF16)], [], 1, "stage", STAGE_FLOPS, MIB)(b_local)
    b_near = exchange(b_local, "row", 1)
    b_last = exchange(b_local, "row", 3)
    (sel,) = call(
        functools.partial(counts_kernel, cols == 2, left_tiles, left_each, right_each),
        [shape((tiles, rows * pairs), BF16)],
        [],
        2,
        "counts",
        2 * tiles * tiles * TASKS * TASKS,
        MIB,
    )(a_index, b_index)

    groups = (2,) if pairs * FLAT * 2 < 4 * MIB else (1, 1)
    raw = shape((right_each * LINES, LANES), F32)
    one = shape((LINES, pairs, LANES), BF16)
    shard_flops = 2 * pairs * LINES * LANES * LANES + 2 * pairs * tiles * FLAT
    acc, a_lines = call(
        functools.partial(own_kernel, (1,), len(a_parts)),
        [shape((tiles, FLAT), F32), shape((left_tiles * LINES, LANES), BF16)],
        [raw, one],
        2 + len(a_parts),
        "own_shard",
        OWN_FLOPS,
        4 * MIB,
    )(sel, *a_parts, b_here)
    (acc,) = call(
        functools.partial(more_kernel, pairs, groups),
        [shape((tiles, FLAT), F32)],
        [raw, shape((LINES, max(groups) * pairs, LANES), BF16)],
        5,
        "near_and_far",
        2 * shard_flops,
        8 * MIB,
    )(sel, a_lines, acc, b_far, b_near)
    results, kept = [], []
    for first_line, lines in ((0, FIRST_LINES), (FIRST_LINES, LINES - FIRST_LINES)):
        width = lines * LANES
        outs = [shape((owned, width), F32)] * 2 + [shape((2 * owned, width), BF16)]
        if not kept:
            outs += [shape((LANES, right_each * LANES), BF16)]
        own, far, sent, *made = call(
            functools.partial(last_kernel, 3 * pairs, first_line),
            outs,
            ([] if kept else [raw]) + [shape((lines, pairs, LANES), BF16)],
            4 + len(kept),
            "last_shard",
            shard_flops * lines // LINES,
            2 * MIB,
        )(sel, a_lines, acc, b_last, *kept)
        kept = kept or made
        arrived = exchange(sent, "layer", 1)
        (joined,) = call(
            join_kernel, [shape((owned, width), BF16)], [], 2, "join_cores", owned * width, MIB
        )(far, arrived)
        results += [own, arrived, exchange(joined, "layer", 2)]
    written, column = [], 0
    for own, arrived, joined in zip(results[0::3], results[1::3], results[2::3]):
        written = call(
            functools.partial(add_kernel, column),
            [shape((owned, FLAT), BF16)],
            [shape(own.shape, BF16)],
            3,
            "add_layers",
            owned * FLAT,
            MIB,
            len(written),
        )(own, arrived, joined, *written)
        column += own.shape[1]
    (out,) = written
    return out.reshape(1, 1, owned, FLAT)


def solution(mesh):
    in_specs = (
        P("row", "layer", "col", None, None),
        P("layer", "row", "col", None, None),
        P("row", "col", "layer", None),
        P("row", "col", "layer", None),
    )
    out_specs = P("row", "col", "layer", None)
    return jax.shard_map(shards, mesh=mesh, in_specs=in_specs, out_specs=out_specs, check_vma=False)
```

```python
import functools

import jax
import jax.numpy as jnp
from jax import lax
from jax.experimental import pallas as pl
from jax.experimental.pallas import tpu as pltpu
from jax.sharding import PartitionSpec as P

TILE = 64
TASKS = 8
FLAT = TILE * TILE
LANES = 128
LINES = FLAT // LANES
ROWS_AT_ONCE = 512
FIRST_LINES = LINES // 2
PARTS = 2
TILES_AT_ONCE = 4
LINES_AT_ONCE = 4
MIB = 1 << 20
OWN_FLOPS = 500 * 10**6
STAGE_FLOPS = 2 * 10**9
F32, BF16 = jnp.float32, jnp.bfloat16
OWNER_ORDER = (0, 2, 3, 1)


def iota(shape, axis):
    return lax.broadcasted_iota(jnp.int32, shape, axis)


def ones_where(hit):
    return jnp.where(hit, 1.0, 0.0).astype(BF16)


def split_inner_order():
    src, dst = iota((LANES, LANES), 0), iota((LANES, LANES), 1)
    half, rest = dst // TILE, dst % TILE
    wanted = half * TILE + 2 * (rest % (TILE // 2)) + rest // (TILE // 2)
    return ones_where(src == wanted)


def twice_on_diagonal(lines):
    low = ones_where(iota(lines.shape, 1) < TILE)
    high = ones_where(iota(lines.shape, 1) >= TILE)
    turned = pltpu.roll(lines, TILE, 1).astype(BF16)
    lines = lines.astype(BF16)
    return jnp.concatenate([lines * low, turned * low, turned * high, lines * high], axis=0)


def loop(count, few, body):
    if count <= few:
        for i in range(count):
            body(i)
    else:
        pl.loop(0, count)(body)


def stage_kernel(*refs):
    for ref, out in zip(refs[:len(refs) // 2], refs[len(refs) // 2:]):
        out[...] = ref[...]


def counts_kernel(swap, left_tiles, left_each, right_each, a_slots, b_slots, sel):
    row, col, layer = lax.axis_index("row"), lax.axis_index("col"), lax.axis_index("layer")
    tiles, pairs = sel.shape
    tasks = tiles * TASKS
    owned = tiles // len(OWNER_ORDER)
    place = iota((tiles, tasks), 0)
    group = place // owned
    owner = jnp.zeros_like(group)
    for g, q in enumerate(OWNER_ORDER):
        owner = jnp.where(group == g, q, owner)
    tile = (owner ^ layer) * owned + place % owned
    mine = jnp.where(iota((tiles, tasks), 1) // TASKS == tile, 1.0, 0.0).astype(BF16)
    entry = iota((2 * TASKS, tasks), 0)
    at = iota((2 * TASKS, tasks), 1) % TASKS
    a_index, b_index = a_slots[...], b_slots[...]
    a_place = a_index ^ (col * left_each) if swap else a_index
    a_place = jnp.where(a_index < left_tiles, a_place, left_tiles)
    b_place = ((b_index // right_each) ^ row) * right_each + b_index % right_each
    spread = jnp.where(at == entry, a_place, 0) + jnp.where(at + TASKS == entry, b_place, 0)
    lists = lax.dot_general(
        mine, spread.astype(F32).astype(BF16), (((1,), (1,)), ((), ())), preferred_element_type=F32
    ).astype(jnp.int32)
    width = min(pairs, 1024)

    def some(part):
        here = iota((tiles, width), 1) + part * width
        total = jnp.zeros((tiles, width), F32)
        for e in range(TASKS):
            a_at, b_at = lists[:, e:e + 1], lists[:, TASKS + e:TASKS + e + 1]
            pair = jnp.where(a_at < left_tiles, b_at * left_tiles + a_at, -1)
            total = total + jnp.where(here == pair, 1.0, 0.0)
        sel[:, pl.ds(pl.multiple_of(part * width, width), width)] = total.astype(BF16)

    loop(pairs // width, 1, some)


def left_lines(a_refs, a_lines):
    order = split_inner_order()
    left_tiles = sum(r.shape[0] for r in a_refs)
    lines_at_once = min(LINES, max(1, ROWS_AT_ONCE // left_tiles))
    for i in range(0, LINES, lines_at_once):
        block = jnp.concatenate(
            [
                r[:, j * LANES:(j + 1) * LANES].astype(F32)
                for j in range(i, i + lines_at_once)
                for r in a_refs
            ],
            axis=0,
        ).astype(BF16)
        got = jnp.dot(block, order, preferred_element_type=F32)
        a_lines[i * left_tiles:(i + lines_at_once) * left_tiles, :] = got.astype(BF16)


def all_products(a_lines, b_ref, raw, prod, first, first_line=0, rights=None):
    right_tiles = b_ref.shape[0]
    left_tiles = a_lines.shape[0] // LINES
    for i in range(LINES if raw is not None else 0):
        raw[i * right_tiles:(i + 1) * right_tiles, :] = b_ref[:, i * LANES:(i + 1) * LANES].astype(F32)
    lines = prod.shape[0]
    lines_at_once = min(lines, max(1, ROWS_AT_ONCE // left_tiles))
    rows = lines_at_once * left_tiles

    def some_tiles(p):
        columns = p * TILES_AT_ONCE * LANES
        columns = columns if isinstance(columns, int) else pl.multiple_of(columns, TILES_AT_ONCE * LANES)
        columns = pl.ds(columns, TILES_AT_ONCE * LANES)
        if raw is None:
            right = rights[:, columns]
        else:
            right = jnp.concatenate(
                [
                    twice_on_diagonal(raw[pl.ds(p * TILES_AT_ONCE + h, LINES, stride=right_tiles), :])
                    for h in range(TILES_AT_ONCE)
                ],
                axis=1,
            )
            if rights is not None:
                rights[:, columns] = right

        def some(part):
            at = first_line * left_tiles + part * rows
            at = at if isinstance(at, int) else pl.multiple_of(at, rows)
            got = jnp.dot(a_lines[pl.ds(at, rows), :], right, preferred_element_type=F32).astype(BF16)
            for j in range(lines_at_once):
                for h in range(TILES_AT_ONCE):
                    to = first + (p * TILES_AT_ONCE + h) * left_tiles
                    to = to if isinstance(to, int) else pl.multiple_of(to, left_tiles)
                    prod[part * lines_at_once + j, pl.ds(to, left_tiles), :] = got[
                        j * left_tiles:(j + 1) * left_tiles, h * LANES:(h + 1) * LANES
                    ]

        loop(lines // lines_at_once, 1, some)

    loop(right_tiles // TILES_AT_ONCE, 8 if lines == lines_at_once else 1, some_tiles)


def chosen_sums(sel, first, count, prod, put):
    for j in range(0, prod.shape[0], LINES_AT_ONCE):
        right = jnp.concatenate([prod[j + i, :count, :] for i in range(LINES_AT_ONCE)], axis=1)
        put(
            slice(j * LANES, (j + LINES_AT_ONCE) * LANES),
            jnp.dot(sel[:, first:first + count], right, preferred_element_type=F32),
        )


def own_kernel(groups, n_left, sel, *refs):
    shards = sum(groups)
    a_refs, b_refs = refs[:n_left], refs[n_left:n_left + shards]
    acc, a_lines, raw, prod = refs[n_left + shards:]
    left_lines(a_refs, a_lines)
    add_shards(0, groups, sel, a_lines, b_refs, None, acc, raw, prod)


def more_kernel(start, groups, sel, a_lines, acc, *refs):
    b_refs, (out, raw, prod) = refs[-4::-1], refs[-3:]
    add_shards(start, groups, sel, a_lines, b_refs, acc, out, raw, prod)


def add_shards(start, groups, sel, a_lines, b_refs, acc, out, raw, prod):
    each = a_lines.shape[0] // LINES
    taken = 0
    for count in groups:
        done = 0
        before = out if taken else acc
        for b_ref in b_refs[taken:taken + count]:
            all_products(a_lines, b_ref, raw, prod, done)
            done += b_ref.shape[0] * each

        def put(columns, value):
            out[:, columns] = value if before is None else value + before[:, columns]

        chosen_sums(sel, start, done, prod, put)
        taken += count
        start += done


def last_kernel(start, first_line, sel, a_lines, acc, b_ref, *refs):
    if first_line:
        (rights, own, far, sent, prod), raw = refs, None
    else:
        own, far, sent, rights, raw, prod = refs
    pairs = b_ref.shape[0] * a_lines.shape[0] // LINES
    owned = own.shape[0]
    lines = prod.shape[0] // PARTS
    for part in range(PARTS):
        skipped = part * lines
        here = prod.at[skipped:skipped + lines]
        all_products(a_lines, b_ref, None if part else raw, here, 0, first_line + skipped, rights)

        def put(columns, value, skipped=skipped):
            columns = slice(columns.start + skipped * LANES, columns.stop + skipped * LANES)
            value = value + acc[:, first_line * LANES + columns.start:first_line * LANES + columns.stop]
            own[:, columns] = value[:owned]
            far[:, columns] = value[owned:2 * owned]
            sent[:, columns] = value[2 * owned:].astype(sent.dtype)

        chosen_sums(sel, start, pairs, here, put)


def join_kernel(far, arrived, out):
    out[...] = (far[...] + arrived[:out.shape[0], :].astype(F32)).astype(out.dtype)


def add_kernel(first_column, own, arrived, joined, *refs):
    out, total, sem = refs[-3:]
    count, width = own.shape
    value = own[...] + arrived[count:, :].astype(F32) + joined[...].astype(F32)
    total[...] = value.astype(total.dtype)
    write = pltpu.make_async_copy(total, out.at[:, pl.ds(first_column, width)], sem)
    write.start()
    write.wait()


VMEM = pl.BlockSpec(memory_space=pltpu.VMEM)
HBM = pl.BlockSpec(memory_space=pltpu.HBM)


def shape(dims, kind):
    return jax.ShapeDtypeStruct(dims, kind)


def call(kernel, outs, scratch, n_in, name, flops, moved, in_place=None):
    held = sum(s.dtype.itemsize * functools.reduce(lambda x, y: x * y, s.shape) for s in outs + scratch)
    return pl.pallas_call(
        kernel,
        out_shape=outs,
        in_specs=[VMEM] * n_in + [HBM] * (in_place or 0),
        out_specs=[VMEM if in_place is None else HBM] * len(outs),
        scratch_shapes=[pltpu.VMEM(s.shape, s.dtype) for s in scratch]
        + ([] if in_place is None else [pltpu.SemaphoreType.DMA]),
        input_output_aliases={n_in: 0} if in_place else {},
        compiler_params=pltpu.CompilerParams(vmem_limit_bytes=min(held + 16 * MIB, 58 * MIB)),
        cost_estimate=pl.CostEstimate(flops=flops, bytes_accessed=moved, transcendentals=0),
        name=name,
    )


def exchange(x, axis, q):
    size = lax.axis_size(axis)
    return lax.ppermute(x, axis, [(i, i ^ q) for i in range(size)])


def shards(a_tiles, b_tiles, a_slots, b_slots):
    a_local = a_tiles.reshape(-1, FLAT)
    b_local = b_tiles.reshape(-1, FLAT)
    a_index = a_slots.reshape(1, -1)
    b_index = b_slots.reshape(1, -1)
    rows, cols, layers = lax.axis_size("row"), lax.axis_size("col"), lax.axis_size("layer")
    left_each, right_each = a_local.shape[0], b_local.shape[0]
    left_tiles = cols * left_each
    tiles = a_index.shape[1] // TASKS
    owned = tiles // layers
    pairs = right_each * left_tiles
    assert rows == 4 and layers == len(OWNER_ORDER)

    b_far = exchange(b_local, "row", 2)
    if cols == 2:
        a_parts = [a_local, exchange(a_local, "col", 1)]
    else:
        a_parts = [lax.all_gather(a_local, "col", axis=0, tiled=True)]
    (b_here,) = call(stage_kernel, [shape(b_local.shape, BF16)], [], 1, "stage", STAGE_FLOPS, MIB)(b_local)
    b_near = exchange(b_local, "row", 1)
    b_last = exchange(b_local, "row", 3)
    (sel,) = call(
        functools.partial(counts_kernel, cols == 2, left_tiles, left_each, right_each),
        [shape((tiles, rows * pairs), BF16)],
        [],
        2,
        "counts",
        2 * tiles * tiles * TASKS * TASKS,
        MIB,
    )(a_index, b_index)

    groups = (2,) if pairs * FLAT * 2 < 4 * MIB else (1, 1)
    raw = shape((right_each * (LINES + 1), LANES), F32)
    one = shape((LINES, pairs, LANES), BF16)
    shard_flops = 2 * pairs * LINES * LANES * LANES + 2 * pairs * tiles * FLAT
    acc, a_lines = call(
        functools.partial(own_kernel, (1,), len(a_parts)),
        [shape((tiles, FLAT), F32), shape((left_tiles * LINES, LANES), BF16)],
        [raw, one],
        2 + len(a_parts),
        "own_shard",
        OWN_FLOPS,
        4 * MIB,
    )(sel, *a_parts, b_here)
    (acc,) = call(
        functools.partial(more_kernel, pairs, groups),
        [shape((tiles, FLAT), F32)],
        [raw, shape((LINES, max(groups) * pairs, LANES), BF16)],
        5,
        "near_and_far",
        2 * shard_flops,
        8 * MIB,
    )(sel, a_lines, acc, b_far, b_near)
    results, kept = [], []
    for first_line, lines in ((0, FIRST_LINES), (FIRST_LINES, LINES - FIRST_LINES)):
        width = lines * LANES
        outs = [shape((owned, width), F32)] * 2 + [shape((2 * owned, width), BF16)]
        if not kept:
            outs += [shape((LANES, right_each * LANES), BF16)]
        own, far, sent, *made = call(
            functools.partial(last_kernel, 3 * pairs, first_line),
            outs,
            ([] if kept else [raw]) + [shape((lines, pairs, LANES), BF16)],
            4 + len(kept),
            "last_shard",
            shard_flops * lines // LINES,
            2 * MIB,
        )(sel, a_lines, acc, b_last, *kept)
        kept = kept or made
        arrived = exchange(sent, "layer", 1)
        (joined,) = call(
            join_kernel, [shape((owned, width), BF16)], [], 2, "join_cores", owned * width, MIB
        )(far, arrived)
        results += [own, arrived, exchange(joined, "layer", 2)]
    written, column = [], 0
    for own, arrived, joined in zip(results[0::3], results[1::3], results[2::3]):
        written = call(
            functools.partial(add_kernel, column),
            [shape((owned, FLAT), BF16)],
            [shape(own.shape, BF16)],
            3,
            "add_layers",
            owned * FLAT,
            MIB,
            len(written),
        )(own, arrived, joined, *written)
        column += own.shape[1]
    (out,) = written
    return out.reshape(1, 1, owned, FLAT)


def solution(mesh):
    in_specs = (
        P("row", "layer", "col", None, None),
        P("layer", "row", "col", None, None),
        P("row", "col", "layer", None),
        P("row", "col", "layer", None),
    )
    out_specs = P("row", "col", "layer", None)
    return jax.shard_map(shards, mesh=mesh, in_specs=in_specs, out_specs=out_specs, check_vma=False)
```

```python
import functools

import jax
import jax.numpy as jnp
from jax import lax
from jax.experimental import pallas as pl
from jax.experimental.pallas import tpu as pltpu
from jax.sharding import PartitionSpec as P

TILE = 64
TASKS = 8
FLAT = TILE * TILE
LANES = 128
LINES = FLAT // LANES
ROWS_AT_ONCE = 512
FIRST_LINES = LINES // 2
TILES_AT_ONCE = 4
LINES_AT_ONCE = 4
MIB = 1 << 20
OWN_FLOPS = 500 * 10**6
STAGE_FLOPS = 2 * 10**9
F32, BF16 = jnp.float32, jnp.bfloat16
OWNER_ORDER = (0, 2, 3, 1)


def iota(shape, axis):
    return lax.broadcasted_iota(jnp.int32, shape, axis)


def ones_where(hit):
    return jnp.where(hit, 1.0, 0.0).astype(BF16)


def split_inner_order():
    src, dst = iota((LANES, LANES), 0), iota((LANES, LANES), 1)
    half, rest = dst // TILE, dst % TILE
    wanted = half * TILE + 2 * (rest % (TILE // 2)) + rest // (TILE // 2)
    return ones_where(src == wanted)


def twice_on_diagonal(lines):
    low = ones_where(iota(lines.shape, 1) < TILE)
    high = ones_where(iota(lines.shape, 1) >= TILE)
    turned = pltpu.roll(lines, TILE, 1).astype(BF16)
    lines = lines.astype(BF16)
    return jnp.concatenate([lines * low, turned * low, turned * high, lines * high], axis=0)


def loop(count, few, body):
    if count <= few:
        for i in range(count):
            body(i)
    else:
        pl.loop(0, count)(body)


def stage_kernel(*refs):
    for ref, out in zip(refs[:len(refs) // 2], refs[len(refs) // 2:]):
        out[...] = ref[...]


def counts_kernel(swap, left_tiles, left_each, right_each, a_slots, b_slots, sel):
    row, col, layer = lax.axis_index("row"), lax.axis_index("col"), lax.axis_index("layer")
    tiles, pairs = sel.shape
    tasks = tiles * TASKS
    owned = tiles // len(OWNER_ORDER)
    place = iota((tiles, tasks), 0)
    group = place // owned
    owner = jnp.zeros_like(group)
    for g, q in enumerate(OWNER_ORDER):
        owner = jnp.where(group == g, q, owner)
    tile = (owner ^ layer) * owned + place % owned
    mine = jnp.where(iota((tiles, tasks), 1) // TASKS == tile, 1.0, 0.0).astype(BF16)
    entry = iota((2 * TASKS, tasks), 0)
    at = iota((2 * TASKS, tasks), 1) % TASKS
    a_index, b_index = a_slots[...], b_slots[...]
    a_place = a_index ^ (col * left_each) if swap else a_index
    a_place = jnp.where(a_index < left_tiles, a_place, left_tiles)
    b_place = ((b_index // right_each) ^ row) * right_each + b_index % right_each
    spread = jnp.where(at == entry, a_place, 0) + jnp.where(at + TASKS == entry, b_place, 0)
    lists = lax.dot_general(
        mine, spread.astype(F32).astype(BF16), (((1,), (1,)), ((), ())), preferred_element_type=F32
    ).astype(jnp.int32)
    width = min(pairs, 1024)

    def some(part):
        here = iota((tiles, width), 1) + part * width
        total = jnp.zeros((tiles, width), F32)
        for e in range(TASKS):
            a_at, b_at = lists[:, e:e + 1], lists[:, TASKS + e:TASKS + e + 1]
            pair = jnp.where(a_at < left_tiles, b_at * left_tiles + a_at, -1)
            total = total + jnp.where(here == pair, 1.0, 0.0)
        sel[:, pl.ds(pl.multiple_of(part * width, width), width)] = total.astype(BF16)

    loop(pairs // width, 1, some)


def left_lines(a_refs, a_lines):
    order = split_inner_order()
    left_tiles = sum(r.shape[0] for r in a_refs)
    lines_at_once = min(LINES, max(1, ROWS_AT_ONCE // left_tiles))
    for i in range(0, LINES, lines_at_once):
        block = jnp.concatenate(
            [
                r[:, j * LANES:(j + 1) * LANES].astype(F32)
                for j in range(i, i + lines_at_once)
                for r in a_refs
            ],
            axis=0,
        ).astype(BF16)
        got = jnp.dot(block, order, preferred_element_type=F32)
        a_lines[i * left_tiles:(i + lines_at_once) * left_tiles, :] = got.astype(BF16)


def all_products(a_lines, b_ref, raw, prod, first, first_line=0, rights=None):
    right_tiles = b_ref.shape[0]
    left_tiles = a_lines.shape[0] // LINES
    for i in range(LINES if raw is not None else 0):
        raw[i * right_tiles:(i + 1) * right_tiles, :] = b_ref[:, i * LANES:(i + 1) * LANES].astype(F32)
    lines = prod.shape[0]
    lines_at_once = min(lines, max(1, ROWS_AT_ONCE // left_tiles))
    rows = lines_at_once * left_tiles

    def some_tiles(p):
        columns = p * TILES_AT_ONCE * LANES
        columns = columns if isinstance(columns, int) else pl.multiple_of(columns, TILES_AT_ONCE * LANES)
        columns = pl.ds(columns, TILES_AT_ONCE * LANES)
        if raw is None:
            right = rights[:, columns]
        else:
            right = jnp.concatenate(
                [
                    twice_on_diagonal(raw[pl.ds(p * TILES_AT_ONCE + h, LINES, stride=right_tiles), :])
                    for h in range(TILES_AT_ONCE)
                ],
                axis=1,
            )
            if rights is not None:
                rights[:, columns] = right

        def some(part):
            at = first_line * left_tiles + part * rows
            at = at if isinstance(at, int) else pl.multiple_of(at, rows)
            got = jnp.dot(a_lines[pl.ds(at, rows), :], right, preferred_element_type=F32).astype(BF16)
            for j in range(lines_at_once):
                for h in range(TILES_AT_ONCE):
                    to = first + (p * TILES_AT_ONCE + h) * left_tiles
                    to = to if isinstance(to, int) else pl.multiple_of(to, left_tiles)
                    prod[part * lines_at_once + j, pl.ds(to, left_tiles), :] = got[
                        j * left_tiles:(j + 1) * left_tiles, h * LANES:(h + 1) * LANES
                    ]

        loop(lines // lines_at_once, 1, some)

    loop(right_tiles // TILES_AT_ONCE, 8 if lines == lines_at_once else 1, some_tiles)


def chosen_sums(sel, first, count, prod, put):
    for j in range(0, prod.shape[0], LINES_AT_ONCE):
        right = jnp.concatenate([prod[j + i, :count, :] for i in range(LINES_AT_ONCE)], axis=1)
        put(
            slice(j * LANES, (j + LINES_AT_ONCE) * LANES),
            jnp.dot(sel[:, first:first + count], right, preferred_element_type=F32),
        )


def own_kernel(groups, n_left, sel, *refs):
    shards = sum(groups)
    a_refs, b_refs = refs[:n_left], refs[n_left:n_left + shards]
    acc, a_lines, raw, prod = refs[n_left + shards:]
    left_lines(a_refs, a_lines)
    add_shards(0, groups, sel, a_lines, b_refs, None, acc, raw, prod)


def more_kernel(start, groups, sel, a_lines, acc, *refs):
    b_refs, (out, raw, prod) = refs[-4::-1], refs[-3:]
    add_shards(start, groups, sel, a_lines, b_refs, acc, out, raw, prod)


def add_shards(start, groups, sel, a_lines, b_refs, acc, out, raw, prod):
    each = a_lines.shape[0] // LINES
    taken = 0
    for count in groups:
        done = 0
        before = out if taken else acc
        for b_ref in b_refs[taken:taken + count]:
            all_products(a_lines, b_ref, raw, prod, done)
            done += b_ref.shape[0] * each

        def put(columns, value):
            out[:, columns] = value if before is None else value + before[:, columns]

        chosen_sums(sel, start, done, prod, put)
        taken += count
        start += done


def last_kernel(start, first_line, sel, a_lines, acc, b_ref, *refs):
    if first_line:
        (rights, own, far, sent, prod), raw = refs, None
    else:
        own, far, sent, rights, raw, prod = refs
    pairs = b_ref.shape[0] * a_lines.shape[0] // LINES
    owned = own.shape[0]
    all_products(a_lines, b_ref, raw, prod, 0, first_line, rights)

    def put(columns, value):
        value = value + acc[:, first_line * LANES + columns.start:first_line * LANES + columns.stop]
        own[:, columns] = value[:owned]
        far[:, columns] = value[owned:2 * owned]
        sent[:, columns] = value[2 * owned:].astype(sent.dtype)

    chosen_sums(sel, start, pairs, prod, put)


def join_kernel(far, arrived, out):
    out[...] = (far[...] + arrived[:out.shape[0], :].astype(F32)).astype(out.dtype)


def add_kernel(first_column, own, arrived, joined, *refs):
    out, total, sem = refs[-3:]
    count, width = own.shape
    value = own[...] + arrived[count:, :].astype(F32) + joined[...].astype(F32)
    total[...] = value.astype(total.dtype)
    write = pltpu.make_async_copy(total, out.at[:, pl.ds(first_column, width)], sem)
    write.start()
    write.wait()


VMEM = pl.BlockSpec(memory_space=pltpu.VMEM)
HBM = pl.BlockSpec(memory_space=pltpu.HBM)


def shape(dims, kind):
    return jax.ShapeDtypeStruct(dims, kind)


def call(kernel, outs, scratch, n_in, name, flops, moved, in_place=None):
    held = sum(s.dtype.itemsize * functools.reduce(lambda x, y: x * y, s.shape) for s in outs + scratch)
    return pl.pallas_call(
        kernel,
        out_shape=outs,
        in_specs=[VMEM] * n_in + [HBM] * (in_place or 0),
        out_specs=[VMEM if in_place is None else HBM] * len(outs),
        scratch_shapes=[pltpu.VMEM(s.shape, s.dtype) for s in scratch]
        + ([] if in_place is None else [pltpu.SemaphoreType.DMA]),
        input_output_aliases={n_in: 0} if in_place else {},
        compiler_params=pltpu.CompilerParams(vmem_limit_bytes=min(held + 16 * MIB, 58 * MIB)),
        cost_estimate=pl.CostEstimate(flops=flops, bytes_accessed=moved, transcendentals=0),
        name=name,
    )


def exchange(x, axis, q):
    size = lax.axis_size(axis)
    return lax.ppermute(x, axis, [(i, i ^ q) for i in range(size)])


def shards(a_tiles, b_tiles, a_slots, b_slots):
    a_local = a_tiles.reshape(-1, FLAT)
    b_local = b_tiles.reshape(-1, FLAT)
    a_index = a_slots.reshape(1, -1)
    b_index = b_slots.reshape(1, -1)
    rows, cols, layers = lax.axis_size("row"), lax.axis_size("col"), lax.axis_size("layer")
    left_each, right_each = a_local.shape[0], b_local.shape[0]
    left_tiles = cols * left_each
    tiles = a_index.shape[1] // TASKS
    owned = tiles // layers
    pairs = right_each * left_tiles
    assert rows == 4 and layers == len(OWNER_ORDER)

    b_far = exchange(b_local, "row", 2)
    if cols == 2:
        a_parts = [a_local, exchange(a_local, "col", 1)]
    else:
        a_parts = [lax.all_gather(a_local, "col", axis=0, tiled=True)]
    (b_here,) = call(stage_kernel, [shape(b_local.shape, BF16)], [], 1, "stage", STAGE_FLOPS, MIB)(b_local)
    b_near = exchange(b_local, "row", 1)
    b_last = exchange(b_local, "row", 3)
    (sel,) = call(
        functools.partial(counts_kernel, cols == 2, left_tiles, left_each, right_each),
        [shape((tiles, rows * pairs), BF16)],
        [],
        2,
        "counts",
        2 * tiles * tiles * TASKS * TASKS,
        MIB,
    )(a_index, b_index)

    groups = (2,) if pairs * FLAT * 2 < 4 * MIB else (1, 1)
    raw = shape((right_each * (LINES + 1), LANES), F32)
    one = shape((LINES, pairs, LANES), BF16)
    shard_flops = 2 * pairs * LINES * LANES * LANES + 2 * pairs * tiles * FLAT
    acc, a_lines = call(
        functools.partial(own_kernel, (1,), len(a_parts)),
        [shape((tiles, FLAT), F32), shape((left_tiles * LINES, LANES), BF16)],
        [raw, one],
        2 + len(a_parts),
        "own_shard",
        OWN_FLOPS,
        4 * MIB,
    )(sel, *a_parts, b_here)
    (acc,) = call(
        functools.partial(more_kernel, pairs, groups),
        [shape((tiles, FLAT), F32)],
        [raw, shape((LINES, max(groups) * pairs, LANES), BF16)],
        5,
        "near_and_far",
        2 * shard_flops,
        8 * MIB,
    )(sel, a_lines, acc, b_far, b_near)
    results, kept = [], []
    for first_line, lines in ((0, FIRST_LINES), (FIRST_LINES, LINES - FIRST_LINES)):
        width = lines * LANES
        outs = [shape((owned, width), F32)] * 2 + [shape((2 * owned, width), BF16)]
        if not kept:
            outs += [shape((LANES, right_each * LANES), BF16)]
        own, far, sent, *made = call(
            functools.partial(last_kernel, 3 * pairs, first_line),
            outs,
            ([] if kept else [raw]) + [shape((lines, pairs, LANES), BF16)],
            4 + len(kept),
            "last_shard",
            shard_flops * lines // LINES,
            2 * MIB,
        )(sel, a_lines, acc, b_last, *kept)
        kept = kept or made
        arrived = exchange(sent, "layer", 1)
        (joined,) = call(
            join_kernel, [shape((owned, width), BF16)], [], 2, "join_cores", owned * width, MIB
        )(far, arrived)
        results += [own, arrived, exchange(joined, "layer", 2)]
    written, column = [], 0
    for own, arrived, joined in zip(results[0::3], results[1::3], results[2::3]):
        written = call(
            functools.partial(add_kernel, column),
            [shape((owned, FLAT), BF16)],
            [shape(own.shape, BF16)],
            3,
            "add_layers",
            owned * FLAT,
            MIB,
            len(written),
        )(own, arrived, joined, *written)
        column += own.shape[1]
    (out,) = written
    return out.reshape(1, 1, owned, FLAT)


def solution(mesh):
    in_specs = (
        P("row", "layer", "col", None, None),
        P("layer", "row", "col", None, None),
        P("row", "col", "layer", None),
        P("row", "col", "layer", None),
    )
    out_specs = P("row", "col", "layer", None)
    return jax.shard_map(shards, mesh=mesh, in_specs=in_specs, out_specs=out_specs, check_vma=False)
```

```python
import functools

import jax
import jax.numpy as jnp
from jax import lax
from jax.experimental import pallas as pl
from jax.experimental.pallas import tpu as pltpu
from jax.sharding import PartitionSpec as P

TILE = 64
TASKS = 8
FLAT = TILE * TILE
LANES = 128
LINES = FLAT // LANES
ROWS_AT_ONCE = 512
FIRST_LINES = LINES // 2
TILES_AT_ONCE = 8
LINES_AT_ONCE = 8
MIB = 1 << 20
OWN_FLOPS = 500 * 10**6
STAGE_FLOPS = 2 * 10**9
F32, BF16 = jnp.float32, jnp.bfloat16
OWNER_ORDER = (0, 2, 3, 1)


def iota(shape, axis):
    return lax.broadcasted_iota(jnp.int32, shape, axis)


def ones_where(hit):
    return jnp.where(hit, 1.0, 0.0).astype(BF16)


def split_inner_order():
    src, dst = iota((LANES, LANES), 0), iota((LANES, LANES), 1)
    half, rest = dst // TILE, dst % TILE
    wanted = half * TILE + 2 * (rest % (TILE // 2)) + rest // (TILE // 2)
    return ones_where(src == wanted)


def twice_on_diagonal(lines):
    low = ones_where(iota(lines.shape, 1) < TILE)
    high = ones_where(iota(lines.shape, 1) >= TILE)
    turned = pltpu.roll(lines, TILE, 1).astype(BF16)
    lines = lines.astype(BF16)
    return jnp.concatenate([lines * low, turned * low, turned * high, lines * high], axis=0)


def loop(count, few, body):
    if count <= few:
        for i in range(count):
            body(i)
    else:
        pl.loop(0, count)(body)


def stage_kernel(*refs):
    for ref, out in zip(refs[:len(refs) // 2], refs[len(refs) // 2:]):
        out[...] = ref[...]


def counts_kernel(swap, left_tiles, left_each, right_each, a_slots, b_slots, sel):
    row, col, layer = lax.axis_index("row"), lax.axis_index("col"), lax.axis_index("layer")
    tiles, pairs = sel.shape
    tasks = tiles * TASKS
    owned = tiles // len(OWNER_ORDER)
    place = iota((tiles, tasks), 0)
    group = place // owned
    owner = jnp.zeros_like(group)
    for g, q in enumerate(OWNER_ORDER):
        owner = jnp.where(group == g, q, owner)
    tile = (owner ^ layer) * owned + place % owned
    mine = jnp.where(iota((tiles, tasks), 1) // TASKS == tile, 1.0, 0.0).astype(BF16)
    entry = iota((2 * TASKS, tasks), 0)
    at = iota((2 * TASKS, tasks), 1) % TASKS
    a_index, b_index = a_slots[...], b_slots[...]
    a_place = a_index ^ (col * left_each) if swap else a_index
    a_place = jnp.where(a_index < left_tiles, a_place, left_tiles)
    b_place = ((b_index // right_each) ^ row) * right_each + b_index % right_each
    spread = jnp.where(at == entry, a_place, 0) + jnp.where(at + TASKS == entry, b_place, 0)
    lists = lax.dot_general(
        mine, spread.astype(F32).astype(BF16), (((1,), (1,)), ((), ())), preferred_element_type=F32
    ).astype(jnp.int32)
    width = min(pairs, 1024)

    def some(part):
        here = iota((tiles, width), 1) + part * width
        total = jnp.zeros((tiles, width), F32)
        for e in range(TASKS):
            a_at, b_at = lists[:, e:e + 1], lists[:, TASKS + e:TASKS + e + 1]
            pair = jnp.where(a_at < left_tiles, b_at * left_tiles + a_at, -1)
            total = total + jnp.where(here == pair, 1.0, 0.0)
        sel[:, pl.ds(pl.multiple_of(part * width, width), width)] = total.astype(BF16)

    loop(pairs // width, 1, some)


def left_lines(a_refs, a_lines):
    order = split_inner_order()
    left_tiles = sum(r.shape[0] for r in a_refs)
    lines_at_once = min(LINES, max(1, ROWS_AT_ONCE // left_tiles))
    for i in range(0, LINES, lines_at_once):
        block = jnp.concatenate(
            [
                r[:, j * LANES:(j + 1) * LANES].astype(F32)
                for j in range(i, i + lines_at_once)
                for r in a_refs
            ],
            axis=0,
        ).astype(BF16)
        got = jnp.dot(block, order, preferred_element_type=F32)
        a_lines[i * left_tiles:(i + lines_at_once) * left_tiles, :] = got.astype(BF16)


def all_products(a_lines, b_ref, raw, prod, first, first_line=0, rights=None):
    right_tiles = b_ref.shape[0]
    left_tiles = a_lines.shape[0] // LINES
    for i in range(LINES if raw is not None else 0):
        raw[i * right_tiles:(i + 1) * right_tiles, :] = b_ref[:, i * LANES:(i + 1) * LANES].astype(F32)
    lines = prod.shape[0]
    lines_at_once = min(lines, max(1, ROWS_AT_ONCE // left_tiles))
    rows = lines_at_once * left_tiles

    def some_tiles(p):
        columns = p * TILES_AT_ONCE * LANES
        columns = columns if isinstance(columns, int) else pl.multiple_of(columns, TILES_AT_ONCE * LANES)
        columns = pl.ds(columns, TILES_AT_ONCE * LANES)
        if raw is None:
            right = rights[:, columns]
        else:
            right = jnp.concatenate(
                [
                    twice_on_diagonal(raw[pl.ds(p * TILES_AT_ONCE + h, LINES, stride=right_tiles), :])
                    for h in range(TILES_AT_ONCE)
                ],
                axis=1,
            )
            if rights is not None:
                rights[:, columns] = right

        def some(part):
            at = first_line * left_tiles + part * rows
            at = at if isinstance(at, int) else pl.multiple_of(at, rows)
            got = jnp.dot(a_lines[pl.ds(at, rows), :], right, preferred_element_type=F32).astype(BF16)
            for j in range(lines_at_once):
                for h in range(TILES_AT_ONCE):
                    to = first + (p * TILES_AT_ONCE + h) * left_tiles
                    to = to if isinstance(to, int) else pl.multiple_of(to, left_tiles)
                    prod[part * lines_at_once + j, pl.ds(to, left_tiles), :] = got[
                        j * left_tiles:(j + 1) * left_tiles, h * LANES:(h + 1) * LANES
                    ]

        loop(lines // lines_at_once, 1, some)

    loop(right_tiles // TILES_AT_ONCE, 8 if lines == lines_at_once else 1, some_tiles)


def chosen_sums(sel, first, count, prod, put):
    for j in range(0, prod.shape[0], LINES_AT_ONCE):
        right = jnp.concatenate([prod[j + i, :count, :] for i in range(LINES_AT_ONCE)], axis=1)
        put(
            slice(j * LANES, (j + LINES_AT_ONCE) * LANES),
            jnp.dot(sel[:, first:first + count], right, preferred_element_type=F32),
        )


def own_kernel(groups, n_left, sel, *refs):
    shards = sum(groups)
    a_refs, b_refs = refs[:n_left], refs[n_left:n_left + shards]
    acc, a_lines, raw, prod = refs[n_left + shards:]
    left_lines(a_refs, a_lines)
    add_shards(0, groups, sel, a_lines, b_refs, None, acc, raw, prod)


def more_kernel(start, groups, sel, a_lines, acc, *refs):
    b_refs, (out, raw, prod) = refs[-4::-1], refs[-3:]
    add_shards(start, groups, sel, a_lines, b_refs, acc, out, raw, prod)


def add_shards(start, groups, sel, a_lines, b_refs, acc, out, raw, prod):
    each = a_lines.shape[0] // LINES
    taken = 0
    for count in groups:
        done = 0
        before = out if taken else acc
        for b_ref in b_refs[taken:taken + count]:
            all_products(a_lines, b_ref, raw, prod, done)
            done += b_ref.shape[0] * each

        def put(columns, value):
            out[:, columns] = value if before is None else value + before[:, columns]

        chosen_sums(sel, start, done, prod, put)
        taken += count
        start += done


def last_kernel(start, first_line, sel, a_lines, acc, b_ref, *refs):
    if first_line:
        (rights, own, far, sent, prod), raw = refs, None
    else:
        own, far, sent, rights, raw, prod = refs
    pairs = b_ref.shape[0] * a_lines.shape[0] // LINES
    owned = own.shape[0]
    all_products(a_lines, b_ref, raw, prod, 0, first_line, rights)

    def put(columns, value):
        value = value + acc[:, first_line * LANES + columns.start:first_line * LANES + columns.stop]
        own[:, columns] = value[:owned]
        far[:, columns] = value[owned:2 * owned]
        sent[:, columns] = value[2 * owned:].astype(sent.dtype)

    chosen_sums(sel, start, pairs, prod, put)


def join_kernel(far, arrived, out):
    out[...] = (far[...] + arrived[:out.shape[0], :].astype(F32)).astype(out.dtype)


def add_kernel(first_column, own, arrived, joined, *refs):
    out, total, sem = refs[-3:]
    count, width = own.shape
    value = own[...] + arrived[count:, :].astype(F32) + joined[...].astype(F32)
    total[...] = value.astype(total.dtype)
    write = pltpu.make_async_copy(total, out.at[:, pl.ds(first_column, width)], sem)
    write.start()
    write.wait()


VMEM = pl.BlockSpec(memory_space=pltpu.VMEM)
HBM = pl.BlockSpec(memory_space=pltpu.HBM)


def shape(dims, kind):
    return jax.ShapeDtypeStruct(dims, kind)


def call(kernel, outs, scratch, n_in, name, flops, moved, in_place=None):
    held = sum(s.dtype.itemsize * functools.reduce(lambda x, y: x * y, s.shape) for s in outs + scratch)
    return pl.pallas_call(
        kernel,
        out_shape=outs,
        in_specs=[VMEM] * n_in + [HBM] * (in_place or 0),
        out_specs=[VMEM if in_place is None else HBM] * len(outs),
        scratch_shapes=[pltpu.VMEM(s.shape, s.dtype) for s in scratch]
        + ([] if in_place is None else [pltpu.SemaphoreType.DMA]),
        input_output_aliases={n_in: 0} if in_place else {},
        compiler_params=pltpu.CompilerParams(vmem_limit_bytes=min(held + 16 * MIB, 58 * MIB)),
        cost_estimate=pl.CostEstimate(flops=flops, bytes_accessed=moved, transcendentals=0),
        name=name,
    )


def exchange(x, axis, q):
    size = lax.axis_size(axis)
    return lax.ppermute(x, axis, [(i, i ^ q) for i in range(size)])


def shards(a_tiles, b_tiles, a_slots, b_slots):
    a_local = a_tiles.reshape(-1, FLAT)
    b_local = b_tiles.reshape(-1, FLAT)
    a_index = a_slots.reshape(1, -1)
    b_index = b_slots.reshape(1, -1)
    rows, cols, layers = lax.axis_size("row"), lax.axis_size("col"), lax.axis_size("layer")
    left_each, right_each = a_local.shape[0], b_local.shape[0]
    left_tiles = cols * left_each
    tiles = a_index.shape[1] // TASKS
    owned = tiles // layers
    pairs = right_each * left_tiles
    assert rows == 4 and layers == len(OWNER_ORDER)

    b_far = exchange(b_local, "row", 2)
    if cols == 2:
        a_parts = [a_local, exchange(a_local, "col", 1)]
    else:
        a_parts = [lax.all_gather(a_local, "col", axis=0, tiled=True)]
    (b_here,) = call(stage_kernel, [shape(b_local.shape, BF16)], [], 1, "stage", STAGE_FLOPS, MIB)(b_local)
    b_near = exchange(b_local, "row", 1)
    b_last = exchange(b_local, "row", 3)
    (sel,) = call(
        functools.partial(counts_kernel, cols == 2, left_tiles, left_each, right_each),
        [shape((tiles, rows * pairs), BF16)],
        [],
        2,
        "counts",
        2 * tiles * tiles * TASKS * TASKS,
        MIB,
    )(a_index, b_index)

    groups = (2,) if pairs * FLAT * 2 < 4 * MIB else (1, 1)
    raw = shape((right_each * (LINES + 1), LANES), F32)
    one = shape((LINES, pairs, LANES), BF16)
    shard_flops = 2 * pairs * LINES * LANES * LANES + 2 * pairs * tiles * FLAT
    acc, a_lines = call(
        functools.partial(own_kernel, (1,), len(a_parts)),
        [shape((tiles, FLAT), F32), shape((left_tiles * LINES, LANES), BF16)],
        [raw, one],
        2 + len(a_parts),
        "own_shard",
        OWN_FLOPS,
        4 * MIB,
    )(sel, *a_parts, b_here)
    (acc,) = call(
        functools.partial(more_kernel, pairs, groups),
        [shape((tiles, FLAT), F32)],
        [raw, shape((LINES, max(groups) * pairs, LANES), BF16)],
        5,
        "near_and_far",
        2 * shard_flops,
        8 * MIB,
    )(sel, a_lines, acc, b_far, b_near)
    results, kept = [], []
    for first_line, lines in ((0, FIRST_LINES), (FIRST_LINES, LINES - FIRST_LINES)):
        width = lines * LANES
        outs = [shape((owned, width), F32)] * 2 + [shape((2 * owned, width), BF16)]
        if not kept:
            outs += [shape((LANES, right_each * LANES), BF16)]
        own, far, sent, *made = call(
            functools.partial(last_kernel, 3 * pairs, first_line),
            outs,
            ([] if kept else [raw]) + [shape((lines, pairs, LANES), BF16)],
            4 + len(kept),
            "last_shard",
            shard_flops * lines // LINES,
            2 * MIB,
        )(sel, a_lines, acc, b_last, *kept)
        kept = kept or made
        arrived = exchange(sent, "layer", 1)
        (joined,) = call(
            join_kernel, [shape((owned, width), BF16)], [], 2, "join_cores", owned * width, MIB
        )(far, arrived)
        results += [own, arrived, exchange(joined, "layer", 2)]
    written, column = [], 0
    for own, arrived, joined in zip(results[0::3], results[1::3], results[2::3]):
        written = call(
            functools.partial(add_kernel, column),
            [shape((owned, FLAT), BF16)],
            [shape(own.shape, BF16)],
            3,
            "add_layers",
            owned * FLAT,
            MIB,
            len(written),
        )(own, arrived, joined, *written)
        column += own.shape[1]
    (out,) = written
    return out.reshape(1, 1, owned, FLAT)


def solution(mesh):
    in_specs = (
        P("row", "layer", "col", None, None),
        P("layer", "row", "col", None, None),
        P("row", "col", "layer", None),
        P("row", "col", "layer", None),
    )
    out_specs = P("row", "col", "layer", None)
    return jax.shard_map(shards, mesh=mesh, in_specs=in_specs, out_specs=out_specs, check_vma=False)
```

```python
import functools

import jax
import jax.numpy as jnp
from jax import lax
from jax.experimental import pallas as pl
from jax.experimental.pallas import tpu as pltpu
from jax.sharding import PartitionSpec as P

TILE = 64
TASKS = 8
FLAT = TILE * TILE
LANES = 128
LINES = FLAT // LANES
ROWS_AT_ONCE = 512
FIRST_LINES = LINES // 2
TILES_AT_ONCE = 8
LINES_AT_ONCE = 8
MIB = 1 << 20
OWN_FLOPS = 500 * 10**6
STAGE_FLOPS = 2 * 10**9
F32, BF16 = jnp.float32, jnp.bfloat16
OWNER_ORDER = (0, 2, 3, 1)


def iota(shape, axis):
    return lax.broadcasted_iota(jnp.int32, shape, axis)


def ones_where(hit):
    return jnp.where(hit, 1.0, 0.0).astype(BF16)


def split_inner_order():
    src, dst = iota((LANES, LANES), 0), iota((LANES, LANES), 1)
    half, rest = dst // TILE, dst % TILE
    wanted = half * TILE + 2 * (rest % (TILE // 2)) + rest // (TILE // 2)
    return ones_where(src == wanted)


def twice_on_diagonal(lines):
    low = ones_where(iota(lines.shape, 1) < TILE)
    high = ones_where(iota(lines.shape, 1) >= TILE)
    turned = pltpu.roll(lines, TILE, 1).astype(BF16)
    lines = lines.astype(BF16)
    return jnp.concatenate([lines * low, turned * low, turned * high, lines * high], axis=0)


def loop(count, few, body):
    if count <= few:
        for i in range(count):
            body(i)
    else:
        pl.loop(0, count)(body)


def stage_kernel(*refs):
    for ref, out in zip(refs[:len(refs) // 2], refs[len(refs) // 2:]):
        out[...] = ref[...]


def counts_kernel(swap, left_tiles, left_each, right_each, a_slots, b_slots, sel):
    row, col, layer = lax.axis_index("row"), lax.axis_index("col"), lax.axis_index("layer")
    tiles, pairs = sel.shape
    tasks = tiles * TASKS
    owned = tiles // len(OWNER_ORDER)
    place = iota((tiles, tasks), 0)
    group = place // owned
    owner = jnp.zeros_like(group)
    for g, q in enumerate(OWNER_ORDER):
        owner = jnp.where(group == g, q, owner)
    tile = (owner ^ layer) * owned + place % owned
    mine = jnp.where(iota((tiles, tasks), 1) // TASKS == tile, 1.0, 0.0).astype(BF16)
    entry = iota((2 * TASKS, tasks), 0)
    at = iota((2 * TASKS, tasks), 1) % TASKS
    a_index, b_index = a_slots[...], b_slots[...]
    a_place = a_index ^ (col * left_each) if swap else a_index
    a_place = jnp.where(a_index < left_tiles, a_place, left_tiles)
    b_place = ((b_index // right_each) ^ row) * right_each + b_index % right_each
    spread = jnp.where(at == entry, a_place, 0) + jnp.where(at + TASKS == entry, b_place, 0)
    lists = lax.dot_general(
        mine, spread.astype(F32).astype(BF16), (((1,), (1,)), ((), ())), preferred_element_type=F32
    ).astype(jnp.int32)
    width = min(pairs, 1024)

    def some(part):
        here = iota((tiles, width), 1) + part * width
        total = jnp.zeros((tiles, width), F32)
        for e in range(TASKS):
            a_at, b_at = lists[:, e:e + 1], lists[:, TASKS + e:TASKS + e + 1]
            pair = jnp.where(a_at < left_tiles, b_at * left_tiles + a_at, -1)
            total = total + jnp.where(here == pair, 1.0, 0.0)
        sel[:, pl.ds(pl.multiple_of(part * width, width), width)] = total.astype(BF16)

    loop(pairs // width, 1, some)


def left_lines(a_refs, a_lines):
    order = split_inner_order()
    left_tiles = sum(r.shape[0] for r in a_refs)
    lines_at_once = min(LINES, max(1, ROWS_AT_ONCE // left_tiles))
    for i in range(0, LINES, lines_at_once):
        block = jnp.concatenate(
            [
                r[:, j * LANES:(j + 1) * LANES].astype(F32)
                for j in range(i, i + lines_at_once)
                for r in a_refs
            ],
            axis=0,
        ).astype(BF16)
        got = jnp.dot(block, order, preferred_element_type=F32)
        a_lines[i * left_tiles:(i + lines_at_once) * left_tiles, :] = got.astype(BF16)


def all_products(a_lines, b_ref, raw, prod, first, first_line=0, rights=None):
    right_tiles = b_ref.shape[0]
    left_tiles = a_lines.shape[0] // LINES
    for i in range(LINES if raw is not None else 0):
        raw[i * right_tiles:(i + 1) * right_tiles, :] = b_ref[:, i * LANES:(i + 1) * LANES].astype(F32)
    lines = prod.shape[0]
    lines_at_once = min(lines, max(1, ROWS_AT_ONCE // left_tiles))
    rows = lines_at_once * left_tiles

    def some_tiles(p):
        columns = p * TILES_AT_ONCE * LANES
        columns = columns if isinstance(columns, int) else pl.multiple_of(columns, TILES_AT_ONCE * LANES)
        columns = pl.ds(columns, TILES_AT_ONCE * LANES)
        if raw is None:
            right = rights[:, columns]
        else:
            right = jnp.concatenate(
                [
                    twice_on_diagonal(raw[pl.ds(p * TILES_AT_ONCE + h, LINES, stride=right_tiles), :])
                    for h in range(TILES_AT_ONCE)
                ],
                axis=1,
            )
            if rights is not None:
                rights[:, columns] = right

        def some(part):
            at = first_line * left_tiles + part * rows
            at = at if isinstance(at, int) else pl.multiple_of(at, rows)
            got = jnp.dot(a_lines[pl.ds(at, rows), :], right, preferred_element_type=F32).astype(BF16)
            for j in range(lines_at_once):
                for h in range(TILES_AT_ONCE):
                    to = first + (p * TILES_AT_ONCE + h) * left_tiles
                    to = to if isinstance(to, int) else pl.multiple_of(to, left_tiles)
                    prod[part * lines_at_once + j, pl.ds(to, left_tiles), :] = got[
                        j * left_tiles:(j + 1) * left_tiles, h * LANES:(h + 1) * LANES
                    ]

        loop(lines // lines_at_once, 1, some)

    loop(right_tiles // TILES_AT_ONCE, 8 if lines == lines_at_once else 1, some_tiles)


def chosen_sums(sel, first, count, prod, put):
    for j in range(0, prod.shape[0], LINES_AT_ONCE):
        right = jnp.concatenate([prod[j + i, :count, :] for i in range(LINES_AT_ONCE)], axis=1)
        put(
            slice(j * LANES, (j + LINES_AT_ONCE) * LANES),
            jnp.dot(sel[:, first:first + count], right, preferred_element_type=F32),
        )


def own_kernel(groups, n_left, sel, *refs):
    shards = sum(groups)
    a_refs, b_refs = refs[:n_left], refs[n_left:n_left + shards]
    acc, a_lines, raw, prod = refs[n_left + shards:]
    left_lines(a_refs, a_lines)
    add_shards(0, groups, sel, a_lines, b_refs, None, acc, raw, prod)


def more_kernel(start, groups, sel, a_lines, acc, *refs):
    b_refs, (out, raw, prod) = refs[-4::-1], refs[-3:]
    add_shards(start, groups, sel, a_lines, b_refs, acc, out, raw, prod)


def add_shards(start, groups, sel, a_lines, b_refs, acc, out, raw, prod):
    each = a_lines.shape[0] // LINES
    taken = 0
    for count in groups:
        done = 0
        before = out if taken else acc
        for b_ref in b_refs[taken:taken + count]:
            all_products(a_lines, b_ref, raw, prod, done)
            done += b_ref.shape[0] * each

        def put(columns, value):
            out[:, columns] = value if before is None else value + before[:, columns]

        chosen_sums(sel, start, done, prod, put)
        taken += count
        start += done


def last_kernel(start, first_line, sel, a_lines, acc, b_ref, *refs):
    if first_line:
        (rights, own, far, sent, prod), raw = refs, None
    else:
        own, far, sent, rights, raw, prod = refs
    pairs = b_ref.shape[0] * a_lines.shape[0] // LINES
    owned = own.shape[0]
    all_products(a_lines, b_ref, raw, prod, 0, first_line, rights)

    def put(columns, value):
        value = value + acc[:, first_line * LANES + columns.start:first_line * LANES + columns.stop]
        own[:, columns] = value[:owned]
        far[:, columns] = value[owned:2 * owned]
        sent[:, columns] = value[2 * owned:].astype(sent.dtype)

    chosen_sums(sel, start, pairs, prod, put)


def join_kernel(far, arrived, out):
    out[...] = (far[...] + arrived[:out.shape[0], :].astype(F32)).astype(out.dtype)


def add_kernel(first_column, own, arrived, joined, *refs):
    out, total, sem = refs[-3:]
    count, width = own.shape
    value = own[...] + arrived[count:, :].astype(F32) + joined[...].astype(F32)
    total[...] = value.astype(total.dtype)
    write = pltpu.make_async_copy(total, out.at[:, pl.ds(first_column, width)], sem)
    write.start()
    write.wait()


VMEM = pl.BlockSpec(memory_space=pltpu.VMEM)
HBM = pl.BlockSpec(memory_space=pltpu.HBM)


def shape(dims, kind):
    return jax.ShapeDtypeStruct(dims, kind)


def call(kernel, outs, scratch, n_in, name, flops, moved, in_place=None):
    held = sum(s.dtype.itemsize * functools.reduce(lambda x, y: x * y, s.shape) for s in outs + scratch)
    return pl.pallas_call(
        kernel,
        out_shape=outs,
        in_specs=[VMEM] * n_in + [HBM] * (in_place or 0),
        out_specs=[VMEM if in_place is None else HBM] * len(outs),
        scratch_shapes=[pltpu.VMEM(s.shape, s.dtype) for s in scratch]
        + ([] if in_place is None else [pltpu.SemaphoreType.DMA]),
        input_output_aliases={n_in: 0} if in_place else {},
        compiler_params=pltpu.CompilerParams(vmem_limit_bytes=min(held + 16 * MIB, 58 * MIB)),
        cost_estimate=pl.CostEstimate(flops=flops, bytes_accessed=moved, transcendentals=0),
        name=name,
    )


def exchange(x, axis, q):
    size = lax.axis_size(axis)
    return lax.ppermute(x, axis, [(i, i ^ q) for i in range(size)])


def shards(a_tiles, b_tiles, a_slots, b_slots):
    a_local = a_tiles.reshape(-1, FLAT)
    b_local = b_tiles.reshape(-1, FLAT)
    a_index = a_slots.reshape(1, -1)
    b_index = b_slots.reshape(1, -1)
    rows, cols, layers = lax.axis_size("row"), lax.axis_size("col"), lax.axis_size("layer")
    left_each, right_each = a_local.shape[0], b_local.shape[0]
    left_tiles = cols * left_each
    tiles = a_index.shape[1] // TASKS
    owned = tiles // layers
    pairs = right_each * left_tiles
    assert rows == 4 and layers == len(OWNER_ORDER)

    b_far = exchange(b_local, "row", 2)
    if cols == 2:
        a_parts = [a_local, exchange(a_local, "col", 1)]
    else:
        a_parts = [lax.all_gather(a_local, "col", axis=0, tiled=True)]
    (b_here,) = call(stage_kernel, [shape(b_local.shape, BF16)], [], 1, "stage", STAGE_FLOPS, MIB)(b_local)
    b_near = exchange(b_here, "row", 1)
    b_last = exchange(b_local, "row", 3)
    (sel,) = call(
        functools.partial(counts_kernel, cols == 2, left_tiles, left_each, right_each),
        [shape((tiles, rows * pairs), BF16)],
        [],
        2,
        "counts",
        2 * tiles * tiles * TASKS * TASKS,
        MIB,
    )(a_index, b_index)

    groups = (2,) if pairs * FLAT * 2 < 4 * MIB else (1, 1)
    raw = shape((right_each * (LINES + 1), LANES), F32)
    one = shape((LINES, pairs, LANES), BF16)
    shard_flops = 2 * pairs * LINES * LANES * LANES + 2 * pairs * tiles * FLAT
    acc, a_lines = call(
        functools.partial(own_kernel, (1,), len(a_parts)),
        [shape((tiles, FLAT), F32), shape((left_tiles * LINES, LANES), BF16)],
        [raw, one],
        2 + len(a_parts),
        "own_shard",
        OWN_FLOPS,
        4 * MIB,
    )(sel, *a_parts, b_here)
    (acc,) = call(
        functools.partial(more_kernel, pairs, groups),
        [shape((tiles, FLAT), F32)],
        [raw, shape((LINES, max(groups) * pairs, LANES), BF16)],
        5,
        "near_and_far",
        2 * shard_flops,
        8 * MIB,
    )(sel, a_lines, acc, b_far, b_near)
    results, kept = [], []
    for first_line, lines in ((0, FIRST_LINES), (FIRST_LINES, LINES - FIRST_LINES)):
        width = lines * LANES
        outs = [shape((owned, width), F32)] * 2 + [shape((2 * owned, width), BF16)]
        if not kept:
            outs += [shape((LANES, right_each * LANES), BF16)]
        own, far, sent, *made = call(
            functools.partial(last_kernel, 3 * pairs, first_line),
            outs,
            ([] if kept else [raw]) + [shape((lines, pairs, LANES), BF16)],
            4 + len(kept),
            "last_shard",
            shard_flops * lines // LINES,
            2 * MIB,
        )(sel, a_lines, acc, b_last, *kept)
        kept = kept or made
        arrived = exchange(sent, "layer", 1)
        (joined,) = call(
            join_kernel, [shape((owned, width), BF16)], [], 2, "join_cores", owned * width, MIB
        )(far, arrived)
        results += [own, arrived, exchange(joined, "layer", 2)]
    written, column = [], 0
    for own, arrived, joined in zip(results[0::3], results[1::3], results[2::3]):
        written = call(
            functools.partial(add_kernel, column),
            [shape((owned, FLAT), BF16)],
            [shape(own.shape, BF16)],
            3,
            "add_layers",
            owned * FLAT,
            MIB,
            len(written),
        )(own, arrived, joined, *written)
        column += own.shape[1]
    (out,) = written
    return out.reshape(1, 1, owned, FLAT)


def solution(mesh):
    in_specs = (
        P("row", "layer", "col", None, None),
        P("layer", "row", "col", None, None),
        P("row", "col", "layer", None),
        P("row", "col", "layer", None),
    )
    out_specs = P("row", "col", "layer", None)
    return jax.shard_map(shards, mesh=mesh, in_specs=in_specs, out_specs=out_specs, check_vma=False)
```
